512 devices in a mesh: src: 16 (over z, core), mod: 32 (over x, y).
Axes of the slice: x: 4, y: 8, z: 8, core: 2. Of those that a mesh axis runs over, the one named last changes fastest.
Arguments:
- right_side: float32 [16, 128, 16, 128], P(None, 'mod'), may hold values from -8 to 8
- depth_weight: float32 [128, 16, 128], P('mod'), may hold values from 0.25 to 2
- panels: bfloat16 [64, 3072, 32, 128], P('src', 'mod'), may hold values from -0.09375 to 0.09375
- data_weight: float32 [64, 3072], P('src', 'mod'), may hold values from 1 to 10
- footprints: int32 [64, 32], replicated, may hold values from 0 to 2047, as said below
- counts: int32 [64], replicated, may hold values from 768 to 3072, as said below
Outputs:
- solution: float32 [16, 128, 16, 128], P(None, 'mod')
- residual: float32 [16, 128, 16, 128], P(None, 'mod')
The draws below stay inside these ranges and needn't reach their ends.
Inputs may be any that keep to these rules, and one draw needn't show every extreme that they name: `footprints`: each row names 32 distinct tiles; at most 2 of one row's tiles lie among the 64 tiles of one index of mod, and in every row some index of mod holds 2 of them. `counts`: some transmitter has all 3072 rows live.
All inputs are finite; a program needn't handle non-finite values.
Results may differ from the reference program's by a relative error of at most 0.039.
Values may be sent and summed in bfloat16 or wider, within the bound.
No kernel may reach another device: no remote copies, remote signals or barrier semaphores. Data moves between devices by JAX's collectives and lax.ppermute only.
A program may use at most 64 MiB of HBM per device.

```python
import math
import jax
import jax.numpy as jnp
from jax import lax

K = 16
BLK = 128
NY = 16
ROWS = 96
ITERS = 3
TX = 64
ROWS_TX = 3072
FOOT = 32
NX = 128
BLK_DEV = 64
N_MOD = 32


def draw_footprints(key, part):
    key = jax.random.fold_in(key, 11)
    key_one, key_two, key_three = jax.random.split(key, 3)
    slot_count = 2 * FOOT
    primary = jax.random.randint(key_one, (TX,), 0, FOOT)
    ranks = jax.vmap(lambda single: jax.random.permutation(single, slot_count))(jax.random.split(key_two, TX))
    slot_ids = jnp.arange(slot_count)
    forced = slot_ids[None, :] // 2 == primary[:, None]
    scores = jnp.where(forced, slot_ids[None, :] % 2, ranks + 2)
    ordering = jnp.argsort(scores, axis=1, stable=True)[:, :FOOT]
    owners = ordering // 2
    base_block = jax.random.randint(key_three, (TX, FOOT), 0, BLK_DEV - 1)
    within = jnp.take_along_axis(base_block, owners, axis=1) + ordering % 2
    return (owners * BLK_DEV + within).astype(jnp.int32)


def draw_counts(key, part):
    key = jax.random.fold_in(key, 23)
    key_one, key_two = jax.random.split(key)
    values = jax.random.randint(key_one, (TX,), ROWS_TX // 4, ROWS_TX + 1)
    top_index = jax.random.randint(key_two, (), 0, TX)
    return jnp.where(jnp.arange(TX) == top_index, ROWS_TX, values).astype(jnp.int32)


def steps_of(stream_key, extent, pieces, least, high):
    level = 1.0
    for axis_at, shards_of in pieces:
        steps = jax.random.uniform(jax.random.fold_in(jax.random.fold_in(stream_key, 6), axis_at), (shards_of,), jnp.float32, least / len(pieces), high / len(pieces))
        level = level * jnp.repeat(jnp.exp(steps), extent[axis_at] // shards_of).reshape((-1,) + (1,) * (len(extent) - 1 - axis_at))
    return level


def bell_draw(own_key, dims, width, most, cuts=(), kind=jnp.bfloat16):
    gain = steps_of(own_key, dims, cuts, -0.22, 0.18) if cuts else 1.0
    array = jax.random.normal(own_key, dims, jnp.float32) * width * gain
    return jnp.minimum(jnp.maximum(array, -most), most).astype(kind)


def setup_inputs(seed: int = 0) -> dict:
    seeds = jax.random.split(jax.random.key(seed), 7)
    right_side = bell_draw(seeds[0], (K, NX, NY, BLK), 1.0, 8.0, ((1, 32),), jnp.float32)
    depth_weight = jnp.clip(0.25 + 1.75 * jax.random.uniform(seeds[1], (NX, NY, BLK), jnp.float32) ** steps_of(seeds[1], (NX, NY, BLK), ((0, 32),), -0.2, 0.2), 0.25, 2.0)
    panels = bell_draw(seeds[2], (TX, ROWS_TX, FOOT, BLK), (FOOT * BLK) ** -0.5, 0.09375, ((0, 16), (1, 32)))
    data_weight = jnp.clip(jnp.exp(math.log(10.0) - 2.3025851 * jax.random.uniform(seeds[3], (TX, ROWS_TX), jnp.float32) ** steps_of(seeds[3], (TX, ROWS_TX), ((0, 16), (1, 32)), -0.2, 0.2)), 1.0, 10.0)
    footprints = draw_footprints(jax.random.fold_in(seeds[6], 71), 0)
    counts = draw_counts(jax.random.fold_in(seeds[6], 71), 0)
    return dict(right_side=right_side, depth_weight=depth_weight, panels=panels, data_weight=data_weight, footprints=footprints, counts=counts)


def solve_small(system, target):
    factor = jnp.linalg.cholesky(system)
    return jax.scipy.linalg.cho_solve((factor, True), target)

def inner_block(first, second):
    columns = first.shape[0]
    return jnp.dot(first.reshape(columns, -1), second.reshape(columns, -1).T, precision=lax.Precision.HIGHEST)

def combine_cols(field, mixing):
    return jnp.einsum('ixyz,ij->jxyz', field, mixing, precision=lax.Precision.HIGHEST)

def regularize(field, depth_weight):
    padded = jnp.pad(field, ((0, 0), (1, 1), (1, 1), (1, 1)))
    beside = padded[:, 2:, 1:-1, 1:-1] + padded[:, :-2, 1:-1, 1:-1]
    beside = beside + padded[:, 1:-1, 2:, 1:-1] + padded[:, 1:-1, :-2, 1:-1]
    beside = beside + padded[:, 1:-1, 1:-1, 2:] + padded[:, 1:-1, 1:-1, :-2]
    return (6.0 + depth_weight)[None] * field - beside

def reference(right_side, depth_weight, panels, data_weight, footprints, counts):
    columns = right_side.shape[0]
    blocks_all = right_side.shape[1] * right_side.shape[2]
    block_len = right_side.shape[3]
    row_ids = jnp.arange(ROWS_TX)

    def apply_data(direction):
        lowered = direction.astype(jnp.bfloat16).reshape(columns, blocks_all, block_len)

        def one(total, inputs):
            panel_t, weight_t, foot_t, count_t = inputs
            picked = jnp.take(lowered, foot_t, axis=1).reshape(columns, FOOT * block_len)
            flat_panel = panel_t.reshape(ROWS_TX, FOOT * block_len)
            response = jnp.dot(flat_panel.astype(jnp.float32), picked.T.astype(jnp.float32), preferred_element_type=jnp.float32)
            live_rows = (row_ids < count_t).astype(jnp.float32)
            weighted = ((weight_t * live_rows)[:, None] * response).astype(jnp.bfloat16)
            shares = jnp.einsum('src,srk->skc', flat_panel.reshape(N_MOD, ROWS, FOOT * block_len).astype(jnp.float32), weighted.reshape(N_MOD, ROWS, columns).astype(jnp.float32), precision=lax.Precision.HIGHEST)
            rounded = lax.optimization_barrier(shares.astype(jnp.bfloat16)).astype(jnp.float32)
            tx_term = jnp.sum(rounded, axis=0).reshape(columns, FOOT, block_len)
            return (total.at[:, foot_t, :].add(tx_term), None)
        zero_sum = jnp.zeros((columns, blocks_all, block_len), jnp.float32)
        total, _ = lax.scan(one, zero_sum, (panels, data_weight, footprints, counts))
        return total.reshape(direction.shape)
    solution = jnp.zeros_like(right_side)
    residual = right_side
    direction = right_side
    norm_now = inner_block(residual, residual)
    for iteration in range(ITERS):
        image = apply_data(direction) + regularize(direction, depth_weight)
        alpha = solve_small(inner_block(direction, image), norm_now)
        solution = solution + combine_cols(direction, alpha)
        residual = residual - combine_cols(image, alpha)
        if iteration + 1 < ITERS:
            norm_next = inner_block(residual, residual)
            beta_block = solve_small(norm_now, norm_next)
            direction = residual + combine_cols(direction, beta_block)
            norm_now = norm_next
    return (solution, residual)
```

```python
import jax
import jax.numpy as jnp
from jax import lax
from jax.sharding import PartitionSpec as P

CAP = 2
ITERS = 3


def solve_small(system, target):
    factor = jnp.linalg.cholesky(system)
    return jax.scipy.linalg.cho_solve((factor, True), target)


def inner_block(first, second):
    return jnp.einsum("lib,ljb->ij", first, second, precision=lax.Precision.HIGHEST)


def combine_cols(field, mixing):
    return jnp.einsum("lib,ij->ljb", field, mixing, precision=lax.Precision.HIGHEST)


def split_three(gram):
    high = lax.reduce_precision(gram, 8, 7)
    rest = gram - high
    middle = lax.reduce_precision(rest, 8, 7)
    low = rest - middle
    parts = jnp.concatenate([high, middle, low], axis=0).astype(jnp.bfloat16)
    return jnp.pad(parts.reshape(-1, 128), ((0, 16 - parts.size // 128), (0, 0)))


def join_three(rows, columns):
    parts = rows.astype(jnp.float32).reshape(rows.shape[0], -1)[:, : 3 * columns * columns]
    return jnp.sum(parts.reshape(-1, columns, columns), axis=0)


def owners_ranks(tile_ids, blocks_dev):
    owners = tile_ids // blocks_dev
    position = jnp.arange(tile_ids.shape[1])
    before = (owners[:, :, None] == owners[:, None, :]) & (
        position[None, None, :] < position[None, :, None]
    )
    ranking = jnp.sum(before.astype(jnp.int32), axis=2)
    return (owners, tile_ids - owners * blocks_dev, ranking)


def to_all(block, axis):
    count = lax.axis_size(axis)
    return lax.all_to_all(
        jnp.broadcast_to(block[None], (count,) + block.shape), axis, 0, 0, tiled=True
    )


def shards(right_side, depth_weight, panels, data_weight, footprints, counts):
    columns, extent_x, extent_y, block_len = right_side.shape
    tx_here, rows_here, foot_len, _ = panels.shape
    mod_count = lax.axis_size("mod")
    src_count = lax.axis_size("src")
    blocks_dev = extent_x * extent_y
    slots = tx_here * CAP
    mod_index = lax.axis_index("mod")
    src_index = lax.axis_index("src")
    group_counts = lax.dynamic_slice_in_dim(counts, src_index * tx_here, tx_here, 0)
    owners_all, within_all, ranking_all = owners_ranks(footprints, blocks_dev)
    mine = lambda ids: lax.dynamic_slice_in_dim(ids, src_index * tx_here, tx_here, 0)
    owners, within, ranking = mine(owners_all), mine(within_all), mine(ranking_all)
    place = owners * slots + jnp.arange(tx_here)[:, None] * CAP + ranking
    spread = (
        place.reshape(-1)[None, :] == jnp.arange(mod_count * slots)[:, None]
    ).astype(jnp.bfloat16)
    chosen = (owners_all == mod_index)[:, None, :] & (
        ranking_all[:, None, :] == jnp.arange(CAP)[None, :, None]
    )
    slot_tile = jnp.min(jnp.where(chosen, within_all[:, None, :], blocks_dev), axis=2)
    scatter = (slot_tile.reshape(-1)[None, :] == jnp.arange(blocks_dev)[:, None]).astype(
        jnp.bfloat16
    )
    own_tile = jnp.minimum(mine(slot_tile).reshape(-1), blocks_dev - 1)
    row_ids = mod_index * rows_here + jnp.arange(rows_here)
    live_rows = (row_ids[None, :] < group_counts[:, None]).astype(jnp.float32)
    row_weight = data_weight * live_rows
    share_of_reg = (src_index == 0).astype(jnp.float32)
    up = [(i, i + 1) for i in range(mod_count - 1)]
    down = [(i + 1, i) for i in range(mod_count - 1)]

    def by_tile(field):
        return field.transpose(1, 2, 0, 3).reshape(blocks_dev, columns, block_len)

    flat_panels = panels.reshape(tx_here, rows_here, foot_len * block_len)
    diagonal = 6.0 + depth_weight.reshape(blocks_dev, 1, block_len)
    residual = by_tile(right_side)
    solution = jnp.zeros_like(residual)
    direction = halo_before = halo_after = response = norm_now = None
    for iteration in range(ITERS):
        low = residual.astype(jnp.bfloat16)
        before = lax.ppermute(low[-extent_y:], "mod", up).astype(jnp.float32)
        after = lax.ppermute(low[:extent_y], "mod", down).astype(jnp.float32)
        picked_here = jnp.take(low, own_tile, axis=0).reshape(slots * columns, block_len)
        sent = jnp.concatenate([picked_here, split_three(inner_block(residual, residual))], axis=0)
        arrived = to_all(sent, "mod")
        norm_next = join_three(arrived[:, slots * columns :], columns)
        picked = jnp.take(
            arrived[:, : slots * columns].reshape(mod_count * slots, columns, block_len),
            place.reshape(-1),
            axis=0,
        )
        picked = picked.reshape(tx_here, foot_len, columns, block_len).transpose(0, 2, 1, 3)
        fresh = jnp.einsum(
            "tkc,trc->tkr",
            picked.reshape(tx_here, columns, -1),
            flat_panels,
            preferred_element_type=jnp.float32,
        )
        if iteration == 0:
            direction, response, halo_before, halo_after = residual, fresh, before, after
        else:
            beta = solve_small(norm_now, norm_next)
            direction = residual + combine_cols(direction, beta)
            halo_before = before + combine_cols(halo_before, beta)
            halo_after = after + combine_cols(halo_after, beta)
            response = fresh + jnp.einsum(
                "tir,ij->tjr", response, beta, precision=lax.Precision.HIGHEST
            )
        norm_now = norm_next
        beside = jnp.concatenate([direction[extent_y:], halo_after], axis=0)
        beside = beside + jnp.concatenate([halo_before, direction[:-extent_y]], axis=0)
        grid = jnp.pad(
            direction.reshape(extent_x, extent_y, columns, block_len),
            ((0, 0), (1, 1), (0, 0), (1, 1)),
        )
        inside = grid[:, 2:, :, 1:-1] + grid[:, :-2, :, 1:-1]
        inside = inside + grid[:, 1:-1, :, 2:] + grid[:, 1:-1, :, :-2]
        smooth = diagonal * direction - beside - inside.reshape(direction.shape)
        weighted_full = row_weight[:, None, :] * response
        curvature_here = jnp.einsum(
            "tir,tjr->ij", response, weighted_full, precision=lax.Precision.HIGHEST
        ) + share_of_reg * inner_block(direction, smooth)
        shares = jnp.einsum(
            "tkr,trc->tkc",
            weighted_full.astype(jnp.bfloat16),
            flat_panels,
            preferred_element_type=jnp.float32,
        ).astype(jnp.bfloat16)
        shares = shares.reshape(tx_here, columns, foot_len, block_len).transpose(0, 2, 1, 3)
        slotted = jnp.dot(
            spread,
            shares.reshape(tx_here * foot_len, columns * block_len),
            preferred_element_type=jnp.float32,
        ).astype(jnp.bfloat16)
        gram_rows = split_three(curvature_here)
        outgoing = jnp.concatenate(
            [
                slotted.reshape(mod_count, slots * columns, block_len),
                jnp.broadcast_to(gram_rows[None], (mod_count,) + gram_rows.shape),
            ],
            axis=1,
        )
        incoming = lax.all_to_all(outgoing, "mod", 0, 0, tiled=True)
        group_sum = jnp.sum(incoming[:, : slots * columns].astype(jnp.float32), axis=0)
        group_gram = join_three(incoming[:, slots * columns :], columns)
        handed = jnp.concatenate(
            [group_sum.astype(jnp.bfloat16), split_three(group_gram)], axis=0
        )
        groups = to_all(handed, "src")
        curvature = join_three(groups[:, slots * columns :], columns)
        data_term = jnp.dot(
            scatter,
            groups[:, : slots * columns].reshape(src_count * slots, columns * block_len),
            preferred_element_type=jnp.float32,
        ).reshape(blocks_dev, columns, block_len)
        image = data_term + smooth
        alpha = solve_small(curvature, norm_now)
        solution = solution + combine_cols(direction, alpha)
        residual = residual - combine_cols(image, alpha)

    def to_field(tiles):
        return tiles.reshape(extent_x, extent_y, columns, block_len).transpose(2, 0, 1, 3)

    return (to_field(solution), to_field(residual))


def solution(mesh):
    placed = (
        P(None, "mod", None, None),
        P("mod", None, None),
        P("src", "mod", None, None),
        P("src", "mod"),
        P(),
        P(),
    )
    return jax.shard_map(
        shards,
        mesh=mesh,
        in_specs=placed,
        out_specs=(P(None, "mod", None, None), P(None, "mod", None, None)),
        check_vma=False,
    )
```

```python
import functools

import jax
import jax.numpy as jnp
from jax import lax
from jax.experimental import pallas as pl
from jax.experimental.pallas import tpu as pltpu
from jax.sharding import PartitionSpec as P

CAP = 2
ITERS = 3
F32 = jnp.float32
BF16 = jnp.bfloat16
VMEM = pl.BlockSpec(memory_space=pltpu.VMEM)
SMEM = pl.BlockSpec(memory_space=pltpu.SMEM)


def call(kernel, outs, args, specs, scratch=(), limit=32 << 20):
    return pl.pallas_call(
        kernel,
        out_shape=[jax.ShapeDtypeStruct(shape, dtype) for shape, dtype in outs],
        in_specs=list(specs),
        out_specs=[VMEM] * len(outs),
        scratch_shapes=list(scratch),
        compiler_params=pltpu.CompilerParams(vmem_limit_bytes=limit),
    )(*args)


def solve_small(system, target):
    size = system.shape[0]
    work = jnp.concatenate([system, target], axis=1)
    rows = lax.broadcasted_iota(jnp.int32, work.shape, 0)
    for j in range(size):
        pivot = work[j : j + 1, :] / work[j : j + 1, j : j + 1]
        work = jnp.where(rows == j, pivot, work - work[:, j : j + 1] * pivot)
    return work[:, size:]


def split_three(gram):
    size = gram.shape[0]
    high = gram.astype(BF16).astype(F32)
    rest = gram - high
    middle = rest.astype(BF16).astype(F32)
    low = rest - middle
    fill = jnp.zeros((size, 128 - 3 * size), F32)
    return jnp.concatenate([high, middle, low, fill], axis=1).astype(BF16)


def join_three(total):
    size = total.shape[0]
    return total[:, :size] + total[:, size : 2 * size] + total[:, 2 * size : 3 * size]


def spread_mixing(mixing):
    size = mixing.shape[0]
    turned = mixing.T
    return [jnp.broadcast_to(turned[:, i : i + 1], (size, 128)) for i in range(size)]


def mix_tile(tile, spread):
    total = None
    for i, factor in enumerate(spread):
        term = factor * tile[i : i + 1, :]
        total = term if total is None else total + term
    return total


def small_dot(first, second, dims):
    return lax.dot_general(
        first, second, (dims, ((), ())), precision=lax.Precision.HIGHEST, preferred_element_type=F32
    )


def halves(value):
    high = value.astype(BF16)
    return high, (value - high.astype(F32)).astype(BF16)


def nt(first, second):
    return lax.dot_general(first, second, (((1,), (1,)), ((), ())), preferred_element_type=F32)


def gram_halves(first, second):
    (fh, fl), (sh, sl) = first, second
    return nt(fh, sh) + (nt(fh, sl) + nt(fl, sh))


def wide(ref, start, count):
    return jnp.concatenate([ref[start + k] for k in range(count)], axis=1)


def gram(first, second):
    tiles, step, total = first.shape[0], 8, None
    for start in range(0, tiles, step):
        one = halves(wide(first, start, step))
        two = one if second is first else halves(wide(second, start, step))
        part = gram_halves(one, two)
        total = part if total is None else total + part
    return total


def pack(residual, own_tile, sent, first_plane, last_plane, copies, slots, plane):
    tiles = residual.shape[0]
    blocks = [residual[own_tile[s]].astype(BF16) for s in range(slots)]
    blocks.append(split_three(gram(residual, residual)))
    for m in range(copies):
        for s in range(slots + 1):
            sent[m * (slots + 1) + s] = blocks[s]
    for y in range(plane):
        first_plane[y] = residual[y].astype(BF16)
        last_plane[y] = residual[tiles - plane + y].astype(BF16)


def begin_kernel(copies, slots, plane, own_tile, residual, sent, first_plane, last_plane):
    pack(residual, own_tile, sent, first_plane, last_plane, copies, slots, plane)


def advance(src_count, slots, slot_tile, groups, residual, smooth, norm, image, fresh):
    tiles = residual.shape[0]
    per = slots + 1
    image[pl.ds(0, tiles)] = smooth[...]

    def add_group(i, curvature):
        for s in range(slots):
            tile = slot_tile[i * slots + s]
            image[tile] = image[tile] + groups[i * per + s].astype(F32)
        return curvature + groups[i * per + slots].astype(F32)

    start = jnp.zeros(groups.shape[1:], F32)
    curvature = join_three(lax.fori_loop(0, src_count, add_group, start))
    alpha = solve_small(curvature, norm[...])
    spread = spread_mixing(alpha)
    for l in range(tiles):
        fresh[l] = residual[l] - mix_tile(image[l], spread)
    return alpha, spread


def step_kernel(
    src_count, copies, slots, plane, slot_tile, own_tile, groups, residual, smooth, norm,
    fresh, alpha_out, sent, first_plane, last_plane, image,
):
    alpha, _ = advance(src_count, slots, slot_tile, groups, residual, smooth, norm, image, fresh)
    alpha_out[...] = alpha
    pack(fresh, own_tile, sent, first_plane, last_plane, copies, slots, plane)


def last_kernel(
    src_count, slots, slot_tile, groups, residual, smooth, norm, direction, solution,
    fresh, solution_out, image,
):
    _, spread = advance(src_count, slots, slot_tile, groups, residual, smooth, norm, image, fresh)
    for l in range(residual.shape[0]):
        solution_out[l] = solution[l] + mix_tile(direction[l], spread)


def smooth_field(field, before, after, diagonal, out, plane):
    tiles = field.shape[0]
    lanes = lax.broadcasted_iota(jnp.int32, field.shape[1:], 1)
    last = field.shape[2] - 1
    for l in range(tiles):
        tile = field[l]
        y = l % plane
        beside = jnp.where(lanes == 0, 0.0, pltpu.roll(tile, 1, 1))
        beside = beside + jnp.where(lanes == last, 0.0, pltpu.roll(tile, last, 1))
        if y > 0:
            beside = beside + field[l - 1]
        if y < plane - 1:
            beside = beside + field[l + 1]
        beside = beside + (field[l - plane] if l >= plane else before[l].astype(F32))
        beside = beside + (
            field[l + plane] if l + plane < tiles else after[l + plane - tiles].astype(F32)
        )
        out[l] = diagonal[l : l + 1, :] * tile - beside


def regularize_first(plane, field, before, after, diagonal, smooth, gram_own):
    smooth_field(field, before, after, diagonal, smooth, plane)
    gram_own[...] = gram(field, smooth)


def regularize_kernel(
    plane, field, before, after, diagonal, smooth_old, direction, solution, alpha,
    smooth, gram_own, gram_cross, solution_out,
):
    smooth_field(field, before, after, diagonal, smooth, plane)
    gram_own[...] = gram(field, smooth)
    gram_cross[...] = gram(field, smooth_old)
    spread = spread_mixing(alpha[...])
    for l in range(field.shape[0]):
        solution_out[l] = solution[l] + mix_tile(direction[l], spread)


def data_kernel(first, copies, slots, share, place, arrived, panels, row_weight, *refs):
    if first:
        gram_own, norm_out, response_out, gram_out, outgoing = refs
    else:
        (gram_own, gram_cross, gram_old, norm_old, response_old,
         norm_out, beta_out, response_out, gram_out, outgoing) = refs
    per = slots + 1
    tx_here, rows_here, width = panels.shape
    columns, block_len = arrived.shape[1:]
    foot_len = width // block_len
    total = arrived[slots].astype(F32)
    for m in range(1, copies):
        total = total + arrived[m * per + slots].astype(F32)
    norm = join_three(total)
    norm_out[...] = norm
    beta = None
    pair = gram_own[...]
    if not first:
        beta = solve_small(norm_old[...], norm)
        beta_out[...] = beta
        cross = small_dot(gram_cross[...], beta, ((1,), (0,)))
        inner = small_dot(gram_old[...], beta, ((1,), (0,)))
        pair = pair + cross + cross.T + small_dot(beta, inner, ((0,), (0,)))
    gram_out[...] = pair
    curvature = share * pair
    empty = jnp.zeros((columns, block_len), BF16)
    for m in range(copies):
        for s in range(slots):
            outgoing[m * per + s] = empty
    for t in range(tx_here):
        picked = jnp.concatenate([arrived[place[t, f]] for f in range(foot_len)], axis=1)
        response = nt(picked, panels[t])
        if not first:
            response = response + small_dot(beta, response_old[t], ((0,), (0,)))
        response_out[t] = response
        weighted = response * row_weight[t : t + 1, :]
        curvature = curvature + gram_halves(halves(response), halves(weighted))
        shares = jnp.dot(weighted.astype(BF16), panels[t], preferred_element_type=F32).astype(BF16)
        for f in range(foot_len):
            outgoing[place[t, f]] = shares[:, f * block_len : (f + 1) * block_len]
    pieces = split_three(curvature)
    for m in range(copies):
        outgoing[m * per + slots] = pieces


def mix_kernel(fresh, smooth_fresh, direction, smooth, beta, direction_out, smooth_out):
    spread = spread_mixing(beta[...])
    for l in range(fresh.shape[0]):
        direction_out[l] = fresh[l] + mix_tile(direction[l], spread)
        smooth_out[l] = smooth_fresh[l] + mix_tile(smooth[l], spread)


def sum_kernel(copies, slots, incoming, handed):
    per = slots + 1
    for s in range(per):
        total = incoming[s].astype(F32)
        for m in range(1, copies):
            total = total + incoming[m * per + s].astype(F32)
        handed[s] = total.astype(BF16) if s < slots else split_three(join_three(total))


def owners_ranks(tile_ids, blocks_dev):
    owners = tile_ids // blocks_dev
    position = jnp.arange(tile_ids.shape[1])
    before = (owners[:, :, None] == owners[:, None, :]) & (
        position[None, None, :] < position[None, :, None]
    )
    ranking = jnp.sum(before.astype(jnp.int32), axis=2)
    return (owners, tile_ids - owners * blocks_dev, ranking)


def shards(right_side, depth_weight, panels, data_weight, footprints, counts):
    columns, extent_x, extent_y, block_len = right_side.shape
    tx_here, rows_here, foot_len, _ = panels.shape
    copies = lax.axis_size("mod")
    src_count = lax.axis_size("src")
    tiles = extent_x * extent_y
    plane = extent_y
    slots = tx_here * CAP
    per = slots + 1
    mod_index = lax.axis_index("mod")
    src_index = lax.axis_index("src")
    group_counts = lax.dynamic_slice_in_dim(counts, src_index * tx_here, tx_here, 0)
    owners_all, within_all, ranking_all = owners_ranks(footprints, tiles)
    mine = lambda ids: lax.dynamic_slice_in_dim(ids, src_index * tx_here, tx_here, 0)
    place = mine(owners_all) * per + jnp.arange(tx_here)[:, None] * CAP + mine(ranking_all)
    chosen = (owners_all == mod_index)[:, None, :] & (
        ranking_all[:, None, :] == jnp.arange(CAP)[None, :, None]
    )
    slot_tile = jnp.min(jnp.where(chosen, within_all[:, None, :], tiles), axis=2)
    own_tile = jnp.minimum(mine(slot_tile).reshape(-1), tiles - 1)
    slot_tile = slot_tile.reshape(-1)
    row_ids = mod_index * rows_here + jnp.arange(rows_here)
    row_weight = data_weight * (row_ids[None, :] < group_counts[:, None]).astype(F32)
    up = [(i, i + 1) for i in range(copies - 1)]
    down = [(i + 1, i) for i in range(copies - 1)]
    flat_panels = panels.reshape(tx_here, rows_here, foot_len * block_len)
    diagonal = 6.0 + depth_weight.reshape(tiles, block_len)
    share = 1.0 / src_count

    field = ((tiles, columns, block_len), F32)
    small = ((columns, columns), F32)
    edge = ((plane, columns, block_len), BF16)
    packet = ((copies * per, columns, block_len), BF16)
    responses = ((tx_here, columns, rows_here), F32)
    image = pltpu.VMEM((tiles + 1, columns, block_len), F32)

    residual = right_side.transpose(1, 2, 0, 3).reshape(field[0])
    sent, first_plane, last_plane = call(
        functools.partial(begin_kernel, copies, slots, plane),
        [packet, edge, edge],
        (own_tile, residual),
        (SMEM, VMEM),
    )
    solution = jnp.zeros_like(residual)
    direction = smooth = norm = response = gram_pair = alpha = None
    for iteration in range(ITERS):
        first = iteration == 0
        arrived = lax.all_to_all(sent, "mod", 0, 0, tiled=True)
        before = lax.ppermute(last_plane, "mod", up)
        after = lax.ppermute(first_plane, "mod", down)
        if first:
            smooth, gram_own = call(
                functools.partial(regularize_first, plane),
                [field, small],
                (residual, before, after, diagonal),
                (VMEM,) * 4,
            )
            direction = residual
            norm, response, gram_pair, outgoing = call(
                functools.partial(data_kernel, True, copies, slots, share),
                [small, responses, small, packet],
                (place, arrived, flat_panels, row_weight, gram_own),
                (SMEM,) + (VMEM,) * 4,
            )
            incoming = lax.all_to_all(outgoing, "mod", 0, 0, tiled=True)
        else:
            smooth_fresh, gram_own, gram_cross, solution = call(
                functools.partial(regularize_kernel, plane),
                [field, small, small, field],
                (residual, before, after, diagonal, smooth, direction, solution, alpha),
                (VMEM,) * 8,
            )
            norm, beta, response, gram_pair, outgoing = call(
                functools.partial(data_kernel, False, copies, slots, share),
                [small, small, responses, small, packet],
                (place, arrived, flat_panels, row_weight, gram_own, gram_cross, gram_pair, norm,
                 response),
                (SMEM,) + (VMEM,) * 8,
            )
            incoming = lax.all_to_all(outgoing, "mod", 0, 0, tiled=True)
            direction, smooth = call(
                mix_kernel,
                [field, field],
                (residual, smooth_fresh, direction, smooth, beta),
                (VMEM,) * 5,
            )
        (handed,) = call(
            functools.partial(sum_kernel, copies, slots),
            [((per, columns, block_len), BF16)],
            (incoming,),
            (VMEM,),
        )
        groups = lax.all_gather(handed, "src", axis=0, tiled=True)
        if iteration + 1 < ITERS:
            residual, alpha, sent, first_plane, last_plane = call(
                functools.partial(step_kernel, src_count, copies, slots, plane),
                [field, small, packet, edge, edge],
                (slot_tile, own_tile, groups, residual, smooth, norm),
                (SMEM, SMEM) + (VMEM,) * 4,
                scratch=(image,),
            )
        else:
            residual, solution = call(
                functools.partial(last_kernel, src_count, slots),
                [field, field],
                (slot_tile, groups, residual, smooth, norm, direction, solution),
                (SMEM,) + (VMEM,) * 6,
                scratch=(image,),
            )

    def to_field(parts):
        return parts.reshape(extent_x, extent_y, columns, block_len).transpose(2, 0, 1, 3)

    return (to_field(solution), to_field(residual))


def solution(mesh):
    placed = (
        P(None, "mod", None, None),
        P("mod", None, None),
        P("src", "mod", None, None),
        P("src", "mod"),
        P(),
        P(),
    )
    return jax.shard_map(
        shards,
        mesh=mesh,
        in_specs=placed,
        out_specs=(P(None, "mod", None, None), P(None, "mod", None, None)),
        check_vma=False,
    )
```

```python
import functools

import jax
import jax.numpy as jnp
from jax import lax
from jax.experimental import pallas as pl
from jax.experimental.pallas import tpu as pltpu
from jax.sharding import PartitionSpec as P

CAP = 2
INNER = 8
ITERS = 3
F32 = jnp.float32
BF16 = jnp.bfloat16
VMEM = pl.BlockSpec(memory_space=pltpu.VMEM)
SMEM = pl.BlockSpec(memory_space=pltpu.SMEM)


def call(kernel, outs, args, specs, scratch=(), limit=32 << 20):
    return pl.pallas_call(
        kernel,
        out_shape=[jax.ShapeDtypeStruct(shape, dtype) for shape, dtype in outs],
        in_specs=list(specs),
        out_specs=[VMEM] * len(outs),
        scratch_shapes=list(scratch),
        compiler_params=pltpu.CompilerParams(vmem_limit_bytes=limit),
    )(*args)


def solve_small(system, target):
    size = system.shape[0]
    work = jnp.concatenate([system, target], axis=1)
    rows = lax.broadcasted_iota(jnp.int32, work.shape, 0)
    for j in range(size):
        pivot = work[j : j + 1, :] / work[j : j + 1, j : j + 1]
        work = jnp.where(rows == j, pivot, work - work[:, j : j + 1] * pivot)
    return work[:, size:]


def split_three(gram):
    size = gram.shape[0]
    high = gram.astype(BF16).astype(F32)
    rest = gram - high
    middle = rest.astype(BF16).astype(F32)
    low = rest - middle
    fill = jnp.zeros((size, 128 - 3 * size), F32)
    return jnp.concatenate([high, middle, low, fill], axis=1).astype(BF16)


def join_three(total):
    size = total.shape[0]
    return total[:, :size] + total[:, size : 2 * size] + total[:, 2 * size : 3 * size]


def spread_mixing(mixing):
    size = mixing.shape[0]
    turned = mixing.T
    return [jnp.broadcast_to(turned[:, i : i + 1], (size, 128)) for i in range(size)]


def mix_tile(tile, spread):
    total = None
    for i, factor in enumerate(spread):
        term = factor * tile[i : i + 1, :]
        total = term if total is None else total + term
    return total


def small_dot(first, second, dims):
    return lax.dot_general(
        first, second, (dims, ((), ())), precision=lax.Precision.HIGHEST, preferred_element_type=F32
    )


def halves(value):
    high = value.astype(BF16)
    return high, (value - high.astype(F32)).astype(BF16)


def nt(first, second):
    return lax.dot_general(first, second, (((1,), (1,)), ((), ())), preferred_element_type=F32)


def gram_halves(first, second):
    (fh, fl), (sh, sl) = first, second
    return nt(fh, sh) + (nt(fh, sl) + nt(fl, sh))


def wide(ref, start, count):
    return jnp.concatenate([ref[start + k] for k in range(count)], axis=1)


def gram(first, second):
    tiles, step, total = first.shape[0], 8, None
    for start in range(0, tiles, step):
        one = halves(wide(first, start, step))
        two = one if second is first else halves(wide(second, start, step))
        part = gram_halves(one, two)
        total = part if total is None else total + part
    return total


def pack(residual, own_tile, sent, first_plane, last_plane, copies, slots, plane):
    tiles = residual.shape[0]
    blocks = [residual[own_tile[s]].astype(BF16) for s in range(slots)]
    blocks.append(split_three(gram(residual, residual)))
    for m in range(copies):
        for s in range(slots + 1):
            sent[m * (slots + 1) + s] = blocks[s]
    for y in range(plane):
        first_plane[y] = residual[y].astype(BF16)
        last_plane[y] = residual[tiles - plane + y].astype(BF16)


def begin_kernel(copies, slots, plane, own_tile, residual, sent, first_plane, last_plane):
    pack(residual, own_tile, sent, first_plane, last_plane, copies, slots, plane)


def advance(src_count, slots, slot_tile, groups, residual, smooth, norm, image, fresh):
    tiles = residual.shape[0]
    per = slots + 1
    image[pl.ds(0, tiles)] = smooth[...]

    def add_group(i, curvature):
        for s in range(slots):
            tile = slot_tile[i * slots + s]
            image[tile] = image[tile] + groups[i * per + s].astype(F32)
        return curvature + groups[i * per + slots].astype(F32)

    start = jnp.zeros(groups.shape[1:], F32)
    curvature = join_three(lax.fori_loop(0, src_count, add_group, start))
    alpha = solve_small(curvature, norm[...])
    spread = spread_mixing(alpha)
    for l in range(tiles):
        fresh[l] = residual[l] - mix_tile(image[l], spread)
    return alpha, spread


def step_kernel(
    src_count, copies, slots, plane, slot_tile, own_tile, groups, residual, smooth, norm,
    fresh, alpha_out, sent, first_plane, last_plane, image,
):
    alpha, _ = advance(src_count, slots, slot_tile, groups, residual, smooth, norm, image, fresh)
    alpha_out[...] = alpha
    pack(fresh, own_tile, sent, first_plane, last_plane, copies, slots, plane)


def last_kernel(
    src_count, slots, slot_tile, groups, residual, smooth, norm, direction, solution,
    fresh, solution_out, image,
):
    _, spread = advance(src_count, slots, slot_tile, groups, residual, smooth, norm, image, fresh)
    for l in range(residual.shape[0]):
        solution_out[l] = solution[l] + mix_tile(direction[l], spread)


def smooth_field(field, before, after, diagonal, out, plane):
    tiles = field.shape[0]
    lanes = lax.broadcasted_iota(jnp.int32, field.shape[1:], 1)
    last = field.shape[2] - 1
    for l in range(tiles):
        tile = field[l]
        y = l % plane
        beside = jnp.where(lanes == 0, 0.0, pltpu.roll(tile, 1, 1))
        beside = beside + jnp.where(lanes == last, 0.0, pltpu.roll(tile, last, 1))
        if y > 0:
            beside = beside + field[l - 1]
        if y < plane - 1:
            beside = beside + field[l + 1]
        beside = beside + (field[l - plane] if l >= plane else before[l].astype(F32))
        beside = beside + (
            field[l + plane] if l + plane < tiles else after[l + plane - tiles].astype(F32)
        )
        out[l] = diagonal[l : l + 1, :] * tile - beside


def regularize_first(plane, field, before, after, diagonal, smooth, gram_own):
    smooth_field(field, before, after, diagonal, smooth, plane)
    gram_own[...] = gram(field, smooth)


def regularize_kernel(
    plane, field, before, after, diagonal, smooth_old, direction, solution, alpha,
    smooth, gram_own, gram_cross, solution_out,
):
    smooth_field(field, before, after, diagonal, smooth, plane)
    gram_own[...] = gram(field, smooth)
    gram_cross[...] = gram(field, smooth_old)
    spread = spread_mixing(alpha[...])
    for l in range(field.shape[0]):
        solution_out[l] = solution[l] + mix_tile(direction[l], spread)


def data_kernel(first, copies, slots, share, place, arrived, panels, row_weight, *refs):
    if first:
        gram_own, norm_out, response_out, gram_out, outgoing = refs
    else:
        (gram_own, gram_cross, gram_old, norm_old, response_old,
         norm_out, beta_out, response_out, gram_out, outgoing) = refs
    per = slots + 1
    tx_here, rows_here, width = panels.shape
    columns, block_len = arrived.shape[1:]
    foot_len = width // block_len
    total = arrived[slots].astype(F32)
    for m in range(1, copies):
        total = total + arrived[m * per + slots].astype(F32)
    norm = join_three(total)
    norm_out[...] = norm
    beta = None
    pair = gram_own[...]
    if not first:
        beta = solve_small(norm_old[...], norm)
        beta_out[...] = beta
        cross = small_dot(gram_cross[...], beta, ((1,), (0,)))
        inner = small_dot(gram_old[...], beta, ((1,), (0,)))
        pair = pair + cross + cross.T + small_dot(beta, inner, ((0,), (0,)))
    gram_out[...] = pair
    curvature = share * pair
    empty = jnp.zeros((columns, block_len), BF16)
    for m in range(copies):
        for s in range(slots):
            outgoing[m * per + s] = empty
    for t in range(tx_here):
        picked = jnp.concatenate([arrived[place[t, f]] for f in range(foot_len)], axis=1)
        response = nt(picked, panels[t])
        if not first:
            response = response + small_dot(beta, response_old[t], ((0,), (0,)))
        response_out[t] = response
        weighted = response * row_weight[t : t + 1, :]
        curvature = curvature + gram_halves(halves(response), halves(weighted))
        shares = jnp.dot(weighted.astype(BF16), panels[t], preferred_element_type=F32).astype(BF16)
        for f in range(foot_len):
            outgoing[place[t, f]] = shares[:, f * block_len : (f + 1) * block_len]
    pieces = split_three(curvature)
    for m in range(copies):
        outgoing[m * per + slots] = pieces


def mix_kernel(fresh, smooth_fresh, direction, smooth, beta, direction_out, smooth_out):
    spread = spread_mixing(beta[...])
    for l in range(fresh.shape[0]):
        direction_out[l] = fresh[l] + mix_tile(direction[l], spread)
        smooth_out[l] = smooth_fresh[l] + mix_tile(smooth[l], spread)


def sum_kernel(copies, blocks, slots, incoming, handed):
    per = slots + 1
    for s in range(blocks * per):
        total = incoming[s].astype(F32)
        for m in range(1, copies):
            total = total + incoming[m * blocks * per + s].astype(F32)
        handed[s] = total.astype(BF16) if s % per < slots else split_three(join_three(total))


def owners_ranks(tile_ids, blocks_dev):
    owners = tile_ids // blocks_dev
    position = jnp.arange(tile_ids.shape[1])
    before = (owners[:, :, None] == owners[:, None, :]) & (
        position[None, None, :] < position[None, :, None]
    )
    ranking = jnp.sum(before.astype(jnp.int32), axis=2)
    return (owners, tile_ids - owners * blocks_dev, ranking)


def shards(right_side, depth_weight, panels, data_weight, footprints, counts):
    columns, extent_x, extent_y, block_len = right_side.shape
    tx_here, rows_here, foot_len, _ = panels.shape
    copies = lax.axis_size("mod")
    src_count = lax.axis_size("src")
    tiles = extent_x * extent_y
    plane = extent_y
    slots = tx_here * CAP
    per = slots + 1
    mod_index = lax.axis_index("mod")
    src_index = lax.axis_index("src")
    group_counts = lax.dynamic_slice_in_dim(counts, src_index * tx_here, tx_here, 0)
    owners_all, within_all, ranking_all = owners_ranks(footprints, tiles)
    mine = lambda ids: lax.dynamic_slice_in_dim(ids, src_index * tx_here, tx_here, 0)
    place = mine(owners_all) * per + jnp.arange(tx_here)[:, None] * CAP + mine(ranking_all)
    chosen = (owners_all == mod_index)[:, None, :] & (
        ranking_all[:, None, :] == jnp.arange(CAP)[None, :, None]
    )
    slot_tile = jnp.min(jnp.where(chosen, within_all[:, None, :], tiles), axis=2)
    own_tile = jnp.minimum(mine(slot_tile).reshape(-1), tiles - 1)
    slot_tile = slot_tile.reshape(-1)
    row_ids = mod_index * rows_here + jnp.arange(rows_here)
    row_weight = data_weight * (row_ids[None, :] < group_counts[:, None]).astype(F32)
    up = [(i, i + 1) for i in range(copies - 1)]
    down = [(i + 1, i) for i in range(copies - 1)]
    flat_panels = panels.reshape(tx_here, rows_here, foot_len * block_len)
    diagonal = 6.0 + depth_weight.reshape(tiles, block_len)
    share = 1.0 / src_count
    inner = INNER
    across_x = copies // inner
    along_y = [[x * inner + y for y in range(inner)] for x in range(across_x)]
    along_x = [[x * inner + y for x in range(across_x)] for y in range(inner)]

    field = ((tiles, columns, block_len), F32)
    small = ((columns, columns), F32)
    edge = ((plane, columns, block_len), BF16)
    packet = ((copies * per, columns, block_len), BF16)
    part = ((inner * per, columns, block_len), BF16)

    def reduced(outgoing):
        halfway = lax.all_to_all(
            outgoing, "mod", 0, 0, tiled=True, axis_index_groups=along_x
        )
        (halfway,) = call(
            functools.partial(sum_kernel, across_x, inner, slots), [part], (halfway,), (VMEM,)
        )
        return lax.all_to_all(halfway, "mod", 0, 0, tiled=True, axis_index_groups=along_y)

    responses = ((tx_here, columns, rows_here), F32)
    image = pltpu.VMEM((tiles + 1, columns, block_len), F32)

    residual = right_side.transpose(1, 2, 0, 3).reshape(field[0])
    sent, first_plane, last_plane = call(
        functools.partial(begin_kernel, inner, slots, plane),
        [part, edge, edge],
        (own_tile, residual),
        (SMEM, VMEM),
    )
    solution = jnp.zeros_like(residual)
    direction = smooth = norm = response = gram_pair = alpha = None
    for iteration in range(ITERS):
        first = iteration == 0
        across = lax.all_to_all(sent, "mod", 0, 0, tiled=True, axis_index_groups=along_y)
        across = jnp.broadcast_to(across[None], (across_x,) + across.shape)
        arrived = lax.all_to_all(
            across.reshape(packet[0]), "mod", 0, 0, tiled=True, axis_index_groups=along_x
        )
        before = lax.ppermute(last_plane, "mod", up)
        after = lax.ppermute(first_plane, "mod", down)
        if first:
            smooth, gram_own = call(
                functools.partial(regularize_first, plane),
                [field, small],
                (residual, before, after, diagonal),
                (VMEM,) * 4,
            )
            direction = residual
            norm, response, gram_pair, outgoing = call(
                functools.partial(data_kernel, True, copies, slots, share),
                [small, responses, small, packet],
                (place, arrived, flat_panels, row_weight, gram_own),
                (SMEM,) + (VMEM,) * 4,
            )
            incoming = reduced(outgoing)
        else:
            smooth_fresh, gram_own, gram_cross, solution = call(
                functools.partial(regularize_kernel, plane),
                [field, small, small, field],
                (residual, before, after, diagonal, smooth, direction, solution, alpha),
                (VMEM,) * 8,
            )
            norm, beta, response, gram_pair, outgoing = call(
                functools.partial(data_kernel, False, copies, slots, share),
                [small, small, responses, small, packet],
                (place, arrived, flat_panels, row_weight, gram_own, gram_cross, gram_pair, norm,
                 response),
                (SMEM,) + (VMEM,) * 8,
            )
            incoming = reduced(outgoing)
            direction, smooth = call(
                mix_kernel,
                [field, field],
                (residual, smooth_fresh, direction, smooth, beta),
                (VMEM,) * 5,
            )
        (handed,) = call(
            functools.partial(sum_kernel, inner, 1, slots),
            [((per, columns, block_len), BF16)],
            (incoming,),
            (VMEM,),
        )
        groups = lax.all_gather(handed, "src", axis=0, tiled=True)
        if iteration + 1 < ITERS:
            residual, alpha, sent, first_plane, last_plane = call(
                functools.partial(step_kernel, src_count, inner, slots, plane),
                [field, small, part, edge, edge],
                (slot_tile, own_tile, groups, residual, smooth, norm),
                (SMEM, SMEM) + (VMEM,) * 4,
                scratch=(image,),
            )
        else:
            residual, solution = call(
                functools.partial(last_kernel, src_count, slots),
                [field, field],
                (slot_tile, groups, residual, smooth, norm, direction, solution),
                (SMEM,) + (VMEM,) * 6,
                scratch=(image,),
            )

    def to_field(parts):
        return parts.reshape(extent_x, extent_y, columns, block_len).transpose(2, 0, 1, 3)

    return (to_field(solution), to_field(residual))


def solution(mesh):
    placed = (
        P(None, "mod", None, None),
        P("mod", None, None),
        P("src", "mod", None, None),
        P("src", "mod"),
        P(),
        P(),
    )
    return jax.shard_map(
        shards,
        mesh=mesh,
        in_specs=placed,
        out_specs=(P(None, "mod", None, None), P(None, "mod", None, None)),
        check_vma=False,
    )
```

```python
import functools

import jax
import jax.numpy as jnp
from jax import lax
from jax.experimental import pallas as pl
from jax.experimental.pallas import tpu as pltpu
from jax.sharding import PartitionSpec as P

CAP = 2
INNER = 8
ITERS = 3
F32 = jnp.float32
BF16 = jnp.bfloat16
VMEM = pl.BlockSpec(memory_space=pltpu.VMEM)
SMEM = pl.BlockSpec(memory_space=pltpu.SMEM)


def call(kernel, outs, args, specs, scratch=(), limit=16 << 20):
    return pl.pallas_call(
        kernel,
        out_shape=[jax.ShapeDtypeStruct(shape, dtype) for shape, dtype in outs],
        in_specs=list(specs),
        out_specs=[VMEM] * len(outs),
        scratch_shapes=list(scratch),
        compiler_params=pltpu.CompilerParams(vmem_limit_bytes=limit),
    )(*args)


def solve_small(system, target):
    size = system.shape[0]
    turned = jnp.concatenate([system, target], axis=0)
    rows = [jnp.broadcast_to(turned[:, i : i + 1], (2 * size, 128)) for i in range(size)]
    for p in range(size):
        base = 8 * ((p + 1) // 8)
        lead = [rows[i][p - (2 * size - rows[i].shape[0])][None, :] for i in range(size)]
        keep = base - (2 * size - rows[0].shape[0])
        pivot = rows[p][keep:] / lead[p]
        rows = [
            pivot if i == p else rows[i][keep:] - lead[i] * pivot for i in range(size)
        ]
    return rows


def matrix_turned(rows):
    lanes = lax.broadcasted_iota(jnp.int32, rows[0].shape, 1)
    total = jnp.zeros(rows[0].shape, F32)
    for i, row in enumerate(rows):
        total = jnp.where(lanes == i, row, total)
    return total[:, : len(rows)]


def split_three(gram):
    size = gram.shape[0]
    high = gram.astype(BF16).astype(F32)
    rest = gram - high
    middle = rest.astype(BF16).astype(F32)
    low = rest - middle
    fill = jnp.zeros((size, 128 - 3 * size), F32)
    return jnp.concatenate([high, middle, low, fill], axis=1).astype(BF16)


def join_three(total):
    size = total.shape[0]
    return total[:, :size] + total[:, size : 2 * size] + total[:, 2 * size : 3 * size]


def read_rows(ref):
    return [ref[i] for i in range(ref.shape[0])]


def mix_tile(tile, spread):
    total = None
    for i, factor in enumerate(spread):
        term = factor * tile[i : i + 1, :]
        total = term if total is None else total + term
    return total


def small_dot(first, second, dims):
    return lax.dot_general(
        first, second, (dims, ((), ())), precision=lax.Precision.HIGHEST, preferred_element_type=F32
    )


def halves(value):
    high = value.astype(BF16)
    return high, (value - high.astype(F32)).astype(BF16)


def nt(first, second):
    return lax.dot_general(first, second, (((1,), (1,)), ((), ())), preferred_element_type=F32)


def gram_halves(first, second):
    (fh, fl), (sh, sl) = first, second
    return nt(fh, sh) + (nt(fh, sl) + nt(fl, sh))


def wide(ref, start, count):
    return jnp.concatenate([ref[start + k] for k in range(count)], axis=1)


def gram(first, second):
    tiles, step, total = first.shape[0], 8, None
    for start in range(0, tiles, step):
        one = halves(wide(first, start, step))
        two = one if second is first else halves(wide(second, start, step))
        part = gram_halves(one, two)
        total = part if total is None else total + part
    return total


def pack(residual, own_tile, sent, first_plane, last_plane, copies, slots, plane):
    tiles = residual.shape[0]
    blocks = [residual[own_tile[s]].astype(BF16) for s in range(slots)]
    blocks.append(split_three(gram(residual, residual)))
    for m in range(copies):
        for s in range(slots + 1):
            sent[m * (slots + 1) + s] = blocks[s]
    for y in range(plane):
        first_plane[y] = residual[y].astype(BF16)
        last_plane[y] = residual[tiles - plane + y].astype(BF16)


def begin_kernel(copies, slots, plane, own_tile, residual, sent, first_plane, last_plane):
    pack(residual, own_tile, sent, first_plane, last_plane, copies, slots, plane)


def advance(src_count, slots, slot_tile, groups, residual, smooth, norm, image, fresh):
    tiles = residual.shape[0]
    per = slots + 1
    image[pl.ds(0, tiles)] = smooth[...]

    def add_group(i, curvature):
        for s in range(slots):
            tile = slot_tile[i * slots + s]
            image[tile] = image[tile] + groups[i * per + s].astype(F32)
        return curvature + groups[i * per + slots].astype(F32)

    start = jnp.zeros(groups.shape[1:], F32)
    curvature = join_three(lax.fori_loop(0, src_count, add_group, start))
    spread = solve_small(curvature, norm[...])
    for l in range(tiles):
        fresh[l] = residual[l] - mix_tile(image[l], spread)
    return spread


def step_kernel(
    src_count, copies, slots, plane, slot_tile, own_tile, groups, residual, smooth, norm,
    fresh, alpha_out, sent, first_plane, last_plane, image,
):
    alpha = advance(src_count, slots, slot_tile, groups, residual, smooth, norm, image, fresh)
    for i, row in enumerate(alpha):
        alpha_out[i] = row
    pack(fresh, own_tile, sent, first_plane, last_plane, copies, slots, plane)


def last_kernel(
    src_count, slots, slot_tile, groups, residual, smooth, norm, direction, solution,
    fresh, solution_out, image,
):
    spread = advance(src_count, slots, slot_tile, groups, residual, smooth, norm, image, fresh)
    for l in range(residual.shape[0]):
        solution_out[l] = solution[l] + mix_tile(direction[l], spread)


def smooth_field(field, before, after, diagonal, out, plane):
    tiles = field.shape[0]
    lanes = lax.broadcasted_iota(jnp.int32, field.shape[1:], 1)
    last = field.shape[2] - 1
    for l in range(tiles):
        tile = field[l]
        y = l % plane
        beside = jnp.where(lanes == 0, 0.0, pltpu.roll(tile, 1, 1))
        beside = beside + jnp.where(lanes == last, 0.0, pltpu.roll(tile, last, 1))
        if y > 0:
            beside = beside + field[l - 1]
        if y < plane - 1:
            beside = beside + field[l + 1]
        beside = beside + (field[l - plane] if l >= plane else before[l].astype(F32))
        beside = beside + (
            field[l + plane] if l + plane < tiles else after[l + plane - tiles].astype(F32)
        )
        out[l] = diagonal[l : l + 1, :] * tile - beside


def regularize_first(plane, field, before, after, diagonal, smooth, gram_own, rim_before, rim_after):
    rim_before[...] = before[...].astype(F32)
    rim_after[...] = after[...].astype(F32)
    smooth_field(field, before, after, diagonal, smooth, plane)
    gram_own[...] = gram(field, smooth)


def regularize_kernel(
    plane, field, before, after, diagonal, smooth_old, gram_own, gram_cross, fresh
):
    gram_cross[...] = gram(field, smooth_old)
    smooth_field(field, before, after, diagonal, fresh, plane)
    gram_own[...] = gram(field, fresh)


def data_kernel(first, copies, slots, share, place, arrived, panels, row_weight, *refs):
    if first:
        gram_own, norm_out, response_out, gram_out, outgoing = refs
    else:
        (gram_own, gram_cross, gram_old, norm_old, response_old,
         norm_out, beta_out, response_out, gram_out, outgoing) = refs
    per = slots + 1
    tx_here, rows_here, width = panels.shape
    columns, block_len = arrived.shape[1:]
    foot_len = width // block_len
    total = arrived[slots].astype(F32)
    for m in range(1, copies):
        total = total + arrived[m * per + slots].astype(F32)
    norm = join_three(total)
    norm_out[...] = norm
    beta = None
    pair = gram_own[...]
    if not first:
        rows = solve_small(norm_old[...], norm)
        for i, row in enumerate(rows):
            beta_out[i] = row
        beta = matrix_turned(rows)
        cross = small_dot(beta, gram_cross[...], ((1,), (1,)))
        inner = small_dot(beta, gram_old[...], ((1,), (0,)))
        pair = pair + cross + cross.T + small_dot(inner, beta, ((1,), (1,)))
    gram_out[...] = pair
    curvature = share * pair
    empty = jnp.zeros((columns, block_len), BF16)
    responses, weights = [], []
    for m in range(copies):
        for s in range(slots):
            outgoing[m * per + s] = empty
    for t in range(tx_here):
        picked = jnp.concatenate([arrived[place[t, f]] for f in range(foot_len)], axis=1)
        response = nt(picked, panels[t])
        if not first:
            response = response + small_dot(beta, response_old[t], ((1,), (0,)))
        response_out[t] = response
        weighted = response * row_weight[t : t + 1, :]
        responses.append(response)
        weights.append(weighted)
    for t in range(tx_here):
        shares = jnp.dot(
            weights[t].astype(BF16), panels[t], preferred_element_type=F32
        ).astype(BF16)
        for f in range(foot_len):
            outgoing[place[t, f]] = shares[:, f * block_len : (f + 1) * block_len]
    curvature = curvature + gram_halves(
        halves(jnp.concatenate(responses, axis=1)), halves(jnp.concatenate(weights, axis=1))
    )
    pieces = split_three(curvature)
    for m in range(copies):
        outgoing[m * per + slots] = pieces


def mix_kernel(
    plane, fresh, before, after, diagonal, direction, rim_before, rim_after, beta,
    direction_out, smooth_out, rim_before_out, rim_after_out,
):
    spread = read_rows(beta)
    for l in range(fresh.shape[0]):
        direction_out[l] = fresh[l] + mix_tile(direction[l], spread)
    for y in range(plane):
        rim_before_out[y] = before[y].astype(F32) + mix_tile(rim_before[y], spread)
        rim_after_out[y] = after[y].astype(F32) + mix_tile(rim_after[y], spread)
    smooth_field(direction_out, rim_before_out, rim_after_out, diagonal, smooth_out, plane)


def gather_kernel(*refs):
    count = (len(refs) - 1) // 2
    directions, alphas, out = refs[:count], refs[count : 2 * count], refs[-1]
    spreads = [read_rows(alpha) for alpha in alphas]
    for l in range(out.shape[0]):
        total = mix_tile(directions[0][l], spreads[0])
        for direction, spread in zip(directions[1:], spreads[1:]):
            total = total + mix_tile(direction[l], spread)
        out[l] = total


def sum_kernel(copies, blocks, slots, incoming, handed):
    per = slots + 1
    for s in range(blocks * per):
        total = incoming[s].astype(F32)
        for m in range(1, copies):
            total = total + incoming[m * blocks * per + s].astype(F32)
        handed[s] = total.astype(BF16) if s % per < slots else split_three(join_three(total))


def owners_ranks(tile_ids, blocks_dev):
    owners = tile_ids // blocks_dev
    position = jnp.arange(tile_ids.shape[1])
    before = (owners[:, :, None] == owners[:, None, :]) & (
        position[None, None, :] < position[None, :, None]
    )
    ranking = jnp.sum(before.astype(jnp.int32), axis=2)
    return (owners, tile_ids - owners * blocks_dev, ranking)


def shards(right_side, depth_weight, panels, data_weight, footprints, counts):
    columns, extent_x, extent_y, block_len = right_side.shape
    tx_here, rows_here, foot_len, _ = panels.shape
    copies = lax.axis_size("mod")
    src_count = lax.axis_size("src")
    tiles = extent_x * extent_y
    plane = extent_y
    slots = tx_here * CAP
    per = slots + 1
    mod_index = lax.axis_index("mod")
    src_index = lax.axis_index("src")
    group_counts = lax.dynamic_slice_in_dim(counts, src_index * tx_here, tx_here, 0)
    owners_all, within_all, ranking_all = owners_ranks(footprints, tiles)
    mine = lambda ids: lax.dynamic_slice_in_dim(ids, src_index * tx_here, tx_here, 0)
    place = mine(owners_all) * per + jnp.arange(tx_here)[:, None] * CAP + mine(ranking_all)
    chosen = (owners_all == mod_index)[:, None, :] & (
        ranking_all[:, None, :] == jnp.arange(CAP)[None, :, None]
    )
    slot_tile = jnp.min(jnp.where(chosen, within_all[:, None, :], tiles), axis=2)
    own_tile = jnp.minimum(mine(slot_tile).reshape(-1), tiles - 1)
    slot_tile = slot_tile.reshape(-1)
    row_ids = mod_index * rows_here + jnp.arange(rows_here)
    row_weight = data_weight * (row_ids[None, :] < group_counts[:, None]).astype(F32)
    up = [(i, i + 1) for i in range(copies - 1)]
    down = [(i + 1, i) for i in range(copies - 1)]
    flat_panels = panels.reshape(tx_here, rows_here, foot_len * block_len)
    diagonal = 6.0 + depth_weight.reshape(tiles, block_len)
    share = 1.0 / src_count
    inner = INNER
    across_x = copies // inner
    along_y = [[x * inner + y for y in range(inner)] for x in range(across_x)]
    along_x = [[x * inner + y for x in range(across_x)] for y in range(inner)]

    field = ((tiles, columns, block_len), F32)
    small = ((columns, columns), F32)
    edge = ((plane, columns, block_len), BF16)
    factors = ((columns, columns, 128), F32)
    rim = ((plane, columns, block_len), F32)
    packet = ((copies * per, columns, block_len), BF16)
    part = ((inner * per, columns, block_len), BF16)

    def reduced(outgoing):
        halfway = lax.all_to_all(
            outgoing, "mod", 0, 0, tiled=True, axis_index_groups=along_x
        )
        (halfway,) = call(
            functools.partial(sum_kernel, across_x, inner, slots), [part], (halfway,), (VMEM,)
        )
        return lax.all_to_all(halfway, "mod", 0, 0, tiled=True, axis_index_groups=along_y)

    responses = ((tx_here, columns, rows_here), F32)
    image = pltpu.VMEM((tiles + 1, columns, block_len), F32)

    residual = right_side.transpose(1, 2, 0, 3).reshape(field[0])
    sent, first_plane, last_plane = call(
        functools.partial(begin_kernel, inner, slots, plane),
        [part, edge, edge],
        (own_tile, residual),
        (SMEM, VMEM),
    )
    direction = smooth = norm = response = gram_pair = rim_before = rim_after = None
    directions, alphas = [], []
    for iteration in range(ITERS):
        across = lax.all_to_all(sent, "mod", 0, 0, tiled=True, axis_index_groups=along_y)
        before = lax.ppermute(last_plane, "mod", up)
        after = lax.ppermute(first_plane, "mod", down)
        across = jnp.broadcast_to(across[None], (across_x,) + across.shape)
        arrived = lax.all_to_all(
            across.reshape(packet[0]), "mod", 0, 0, tiled=True, axis_index_groups=along_x
        )
        if iteration == 0:
            smooth, gram_own, rim_before, rim_after = call(
                functools.partial(regularize_first, plane),
                [field, small, rim, rim],
                (residual, before, after, diagonal),
                (VMEM,) * 4,
            )
            direction = residual
            norm, response, gram_pair, outgoing = call(
                functools.partial(data_kernel, True, copies, slots, share),
                [small, responses, small, packet],
                (place, arrived, flat_panels, row_weight, gram_own),
                (SMEM,) + (VMEM,) * 4,
            )
            incoming = reduced(outgoing)
        else:
            gram_own, gram_cross = call(
                functools.partial(regularize_kernel, plane),
                [small, small],
                (residual, before, after, diagonal, smooth),
                (VMEM,) * 5,
                scratch=(pltpu.VMEM(field[0], F32),),
            )
            norm, beta, response, gram_pair, outgoing = call(
                functools.partial(data_kernel, False, copies, slots, share),
                [small, factors, responses, small, packet],
                (place, arrived, flat_panels, row_weight, gram_own, gram_cross,
                 gram_pair, norm, response),
                (SMEM,) + (VMEM,) * 8,
            )
            incoming = reduced(outgoing)
            direction, smooth, rim_before, rim_after = call(
                functools.partial(mix_kernel, plane),
                [field, field, rim, rim],
                (residual, before, after, diagonal,
                 direction, rim_before,
                 rim_after, beta),
                (VMEM,) * 8,
            )
        directions.append(direction)
        if iteration + 1 == ITERS:
            (solution,) = call(
                gather_kernel,
                [field],
                (*directions[:-1],
                 *alphas),
                (VMEM,) * (2 * len(alphas)),
            )
        (handed,) = call(
            functools.partial(sum_kernel, inner, 1, slots),
            [((per, columns, block_len), BF16)],
            (incoming,),
            (VMEM,),
        )
        groups = lax.all_gather(handed, "src", axis=0, tiled=True)
        if iteration + 1 < ITERS:
            residual, alpha, sent, first_plane, last_plane = call(
                functools.partial(step_kernel, src_count, inner, slots, plane),
                [field, factors, part, edge, edge],
                (slot_tile, own_tile, groups, residual, smooth, norm),
                (SMEM, SMEM) + (VMEM,) * 4,
                scratch=(image,),
            )
            alphas.append(alpha)
        else:
            residual, solution = call(
                functools.partial(last_kernel, src_count, slots),
                [field, field],
                (slot_tile, groups, residual, smooth, norm, direction,
                 solution),
                (SMEM,) + (VMEM,) * 6,
                scratch=(image,),
            )

    def to_field(parts):
        return parts.reshape(extent_x, extent_y, columns, block_len).transpose(2, 0, 1, 3)

    return (to_field(solution), to_field(residual))


def solution(mesh):
    placed = (
        P(None, "mod", None, None),
        P("mod", None, None),
        P("src", "mod", None, None),
        P("src", "mod"),
        P(),
        P(),
    )
    return jax.shard_map(
        shards,
        mesh=mesh,
        in_specs=placed,
        out_specs=(P(None, "mod", None, None), P(None, "mod", None, None)),
        check_vma=False,
    )
```

```python
import functools

import jax
import jax.numpy as jnp
from jax import lax
from jax.experimental import pallas as pl
from jax.experimental.pallas import tpu as pltpu
from jax.sharding import PartitionSpec as P

CAP = 2
INNER = 8
NARROW = 48
ITERS = 3
F32 = jnp.float32
BF16 = jnp.bfloat16
VMEM = pl.BlockSpec(memory_space=pltpu.VMEM)
SMEM = pl.BlockSpec(memory_space=pltpu.SMEM)


def call(kernel, outs, args, specs, scratch=(), limit=16 << 20):
    return pl.pallas_call(
        kernel,
        out_shape=[jax.ShapeDtypeStruct(shape, dtype) for shape, dtype in outs],
        in_specs=list(specs),
        out_specs=[VMEM] * len(outs),
        scratch_shapes=list(scratch),
        compiler_params=pltpu.CompilerParams(vmem_limit_bytes=limit),
    )(*args)


def solve_small(system, target):
    size = system.shape[0]
    turned = jnp.concatenate([system, target], axis=0)
    rows = [jnp.broadcast_to(turned[:, i : i + 1], (2 * size, 128)) for i in range(size)]
    for p in range(size):
        base = 8 * ((p + 1) // 8)
        lead = [rows[i][p - (2 * size - rows[i].shape[0])][None, :] for i in range(size)]
        keep = base - (2 * size - rows[0].shape[0])
        pivot = rows[p][keep:] / lead[p]
        rows = [
            pivot if i == p else rows[i][keep:] - lead[i] * pivot for i in range(size)
        ]
    return rows


def matrix_turned(rows):
    lanes = lax.broadcasted_iota(jnp.int32, rows[0].shape, 1)
    total = jnp.zeros(rows[0].shape, F32)
    for i, row in enumerate(rows):
        total = jnp.where(lanes == i, row, total)
    return total[:, : len(rows)]


def split_three(gram):
    size = gram.shape[0]
    high = gram.astype(BF16).astype(F32)
    rest = gram - high
    middle = rest.astype(BF16).astype(F32)
    low = rest - middle
    fill = jnp.zeros((size, 128 - 3 * size), F32)
    return jnp.concatenate([high, middle, low, fill], axis=1).astype(BF16)


def join_three(total):
    size = total.shape[0]
    return total[:, :size] + total[:, size : 2 * size] + total[:, 2 * size : 3 * size]


def read_rows(ref):
    return [ref[i] for i in range(ref.shape[0])]


def mix_tile(tile, spread):
    total = None
    for i, factor in enumerate(spread):
        term = factor * tile[i : i + 1, :]
        total = term if total is None else total + term
    return total


def small_dot(first, second, dims):
    return lax.dot_general(
        first, second, (dims, ((), ())), precision=lax.Precision.HIGHEST, preferred_element_type=F32
    )


def halves(value):
    high = value.astype(BF16)
    return high, (value - high.astype(F32)).astype(BF16)


def nt(first, second):
    return lax.dot_general(first, second, (((1,), (1,)), ((), ())), preferred_element_type=F32)


def gram_halves(first, second):
    (fh, fl), (sh, sl) = first, second
    return nt(fh, sh) + (nt(fh, sl) + nt(fl, sh))


def wide(ref, start, count):
    return jnp.concatenate([ref[start + k] for k in range(count)], axis=1)


def gram(first, second):
    tiles, step, total = first.shape[0], 8, None
    for start in range(0, tiles, step):
        one = halves(wide(first, start, step))
        two = one if second is first else halves(wide(second, start, step))
        part = gram_halves(one, two)
        total = part if total is None else total + part
    return total


def pack(residual, own_tile, sent, first_plane, last_plane, copies, slots, plane):
    tiles = residual.shape[0]
    blocks = [residual[own_tile[s]].astype(BF16) for s in range(slots)]
    blocks.append(split_three(gram(residual, residual)))
    for m in range(copies):
        for s in range(slots + 1):
            sent[m * (slots + 1) + s] = blocks[s]
    for y in range(plane):
        first_plane[y] = residual[y].astype(BF16)
        last_plane[y] = residual[tiles - plane + y].astype(BF16)


def begin_kernel(copies, slots, plane, own_tile, residual, sent, first_plane, last_plane):
    pack(residual, own_tile, sent, first_plane, last_plane, copies, slots, plane)


def advance(src_count, slots, slot_tile, groups, residual, smooth, norm, image, fresh):
    tiles = residual.shape[0]
    per = slots + 1
    image[pl.ds(0, tiles)] = smooth[...]

    def add_group(i, curvature):
        for s in range(slots):
            tile = slot_tile[i * slots + s]
            image[tile] = image[tile] + groups[i * per + s].astype(F32)
        return curvature + groups[i * per + slots].astype(F32)

    start = jnp.zeros(groups.shape[1:], F32)
    curvature = join_three(lax.fori_loop(0, src_count, add_group, start))
    spread = solve_small(curvature, norm[...])
    for l in range(tiles):
        fresh[l] = residual[l] - mix_tile(image[l], spread)
    return spread


def step_kernel(
    src_count, copies, slots, plane, slot_tile, own_tile, groups, residual, smooth, norm,
    fresh, alpha_out, sent, first_plane, last_plane, image,
):
    alpha = advance(src_count, slots, slot_tile, groups, residual, smooth, norm, image, fresh)
    for i, row in enumerate(alpha):
        alpha_out[i] = row
    pack(fresh, own_tile, sent, first_plane, last_plane, copies, slots, plane)


def last_kernel(
    src_count, slots, slot_tile, groups, residual, smooth, norm, direction, solution,
    fresh, solution_out, image,
):
    spread = advance(src_count, slots, slot_tile, groups, residual, smooth, norm, image, fresh)
    for l in range(residual.shape[0]):
        solution_out[l] = solution[l] + mix_tile(direction[l], spread)


def smooth_field(field, before, after, diagonal, out, plane):
    tiles = field.shape[0]
    lanes = lax.broadcasted_iota(jnp.int32, field.shape[1:], 1)
    last = field.shape[2] - 1
    for l in range(tiles):
        tile = field[l]
        y = l % plane
        beside = jnp.where(lanes == 0, 0.0, pltpu.roll(tile, 1, 1))
        beside = beside + jnp.where(lanes == last, 0.0, pltpu.roll(tile, last, 1))
        if y > 0:
            beside = beside + field[l - 1]
        if y < plane - 1:
            beside = beside + field[l + 1]
        beside = beside + (field[l - plane] if l >= plane else before[l].astype(F32))
        beside = beside + (
            field[l + plane] if l + plane < tiles else after[l + plane - tiles].astype(F32)
        )
        out[l] = diagonal[l : l + 1, :] * tile - beside


def regularize_first(plane, field, before, after, diagonal, smooth, gram_own, rim_before, rim_after):
    rim_before[...] = before[...].astype(F32)
    rim_after[...] = after[...].astype(F32)
    smooth_field(field, before, after, diagonal, smooth, plane)
    gram_own[...] = gram(field, smooth)


def regularize_kernel(
    plane, field, before, after, diagonal, smooth_old, gram_own, gram_cross, fresh
):
    gram_cross[...] = gram(field, smooth_old)
    smooth_field(field, before, after, diagonal, fresh, plane)
    gram_own[...] = gram(field, fresh)


def data_kernel(first, across_x, cap, share, place, arrived, panels, row_weight, *refs):
    if first:
        gram_own, norm_out, response_out, gram_out, outgoing = refs
    else:
        (gram_own, gram_cross, gram_old, norm_old, response_old,
         norm_out, beta_out, response_out, gram_out, outgoing) = refs
    per = cap + 1
    tx_here, rows_here, width = panels.shape
    columns, block_len = arrived.shape[1:]
    foot_len = width // block_len
    total = arrived[cap].astype(F32)
    for x in range(1, across_x):
        total = total + arrived[x * per + cap].astype(F32)
    norm = join_three(total)
    norm_out[...] = norm
    beta = None
    pair = gram_own[...]
    if not first:
        rows = solve_small(norm_old[...], norm)
        for i, row in enumerate(rows):
            beta_out[i] = row
        beta = matrix_turned(rows)
        cross = small_dot(beta, gram_cross[...], ((1,), (1,)))
        inner = small_dot(beta, gram_old[...], ((1,), (0,)))
        pair = pair + cross + cross.T + small_dot(inner, beta, ((1,), (1,)))
    gram_out[...] = pair
    curvature = share * pair
    empty = jnp.zeros((columns, block_len), BF16)
    responses, weights = [], []
    for x in range(across_x):
        for s in range(cap):
            outgoing[x * per + s] = empty
    for t in range(tx_here):
        picked = jnp.concatenate([arrived[place[t, f]] for f in range(foot_len)], axis=1)
        response = nt(picked, panels[t])
        if not first:
            response = response + small_dot(beta, response_old[t], ((1,), (0,)))
        response_out[t] = response
        weighted = response * row_weight[t : t + 1, :]
        responses.append(response)
        weights.append(weighted)
    for t in range(tx_here):
        shares = jnp.dot(
            weights[t].astype(BF16), panels[t], preferred_element_type=F32
        ).astype(BF16)
        for f in range(foot_len):
            outgoing[place[t, f]] = shares[:, f * block_len : (f + 1) * block_len]
    curvature = curvature + gram_halves(
        halves(jnp.concatenate(responses, axis=1)), halves(jnp.concatenate(weights, axis=1))
    )
    pieces = split_three(curvature)
    for x in range(across_x):
        outgoing[x * per + cap] = pieces


def mix_kernel(
    plane, fresh, before, after, diagonal, direction, rim_before, rim_after, beta,
    direction_out, smooth_out, rim_before_out, rim_after_out,
):
    spread = read_rows(beta)
    for l in range(fresh.shape[0]):
        direction_out[l] = fresh[l] + mix_tile(direction[l], spread)
    for y in range(plane):
        rim_before_out[y] = before[y].astype(F32) + mix_tile(rim_before[y], spread)
        rim_after_out[y] = after[y].astype(F32) + mix_tile(rim_after[y], spread)
    smooth_field(direction_out, rim_before_out, rim_after_out, diagonal, smooth_out, plane)


def gather_kernel(*refs):
    count = (len(refs) - 1) // 2
    directions, alphas, out = refs[:count], refs[count : 2 * count], refs[-1]
    spreads = [read_rows(alpha) for alpha in alphas]
    for l in range(out.shape[0]):
        total = mix_tile(directions[0][l], spreads[0])
        for direction, spread in zip(directions[1:], spreads[1:]):
            total = total + mix_tile(direction[l], spread)
        out[l] = total


def narrow_kernel(across_x, inner, slots, cap, kept, across, out):
    per = slots + 1
    total = across[slots].astype(F32)
    for y in range(1, inner):
        total = total + across[y * per + slots].astype(F32)
    pieces = split_three(join_three(total))
    for x in range(across_x):
        out[x * (cap + 1) + cap] = pieces
    for d in range(cap):
        block = across[kept[d]]
        for x in range(across_x):
            out[x * (cap + 1) + d] = block


def widen_kernel(across_x, inner, slots, cap, kept, incoming, out):
    per = slots + 1
    empty = jnp.zeros(out.shape[1:], BF16)
    for s in range(inner * per):
        out[s] = empty

    def summed(d):
        total = incoming[d].astype(F32)
        for x in range(1, across_x):
            total = total + incoming[x * (cap + 1) + d].astype(F32)
        return total

    for d in range(cap):
        out[kept[d]] = summed(d).astype(BF16)
    pieces = split_three(join_three(summed(cap)))
    for y in range(inner):
        out[y * per + slots] = pieces


def sum_kernel(copies, slots, incoming, handed):
    per = slots + 1
    for s in range(per):
        total = incoming[s].astype(F32)
        for m in range(1, copies):
            total = total + incoming[m * per + s].astype(F32)
        handed[s] = total.astype(BF16) if s < slots else split_three(join_three(total))


def owners_ranks(tile_ids, blocks_dev):
    owners = tile_ids // blocks_dev
    position = jnp.arange(tile_ids.shape[1])
    before = (owners[:, :, None] == owners[:, None, :]) & (
        position[None, None, :] < position[None, :, None]
    )
    ranking = jnp.sum(before.astype(jnp.int32), axis=2)
    return (owners, tile_ids - owners * blocks_dev, ranking)


def shards(right_side, depth_weight, panels, data_weight, footprints, counts):
    columns, extent_x, extent_y, block_len = right_side.shape
    tx_here, rows_here, foot_len, _ = panels.shape
    copies = lax.axis_size("mod")
    src_count = lax.axis_size("src")
    tiles = extent_x * extent_y
    plane = extent_y
    slots = tx_here * CAP
    per = slots + 1
    mod_index = lax.axis_index("mod")
    src_index = lax.axis_index("src")
    group_counts = lax.dynamic_slice_in_dim(counts, src_index * tx_here, tx_here, 0)
    owners_all, within_all, ranking_all = owners_ranks(footprints, tiles)
    mine = lambda ids: lax.dynamic_slice_in_dim(ids, src_index * tx_here, tx_here, 0)
    chosen = (owners_all == mod_index)[:, None, :] & (
        ranking_all[:, None, :] == jnp.arange(CAP)[None, :, None]
    )
    slot_tile = jnp.min(jnp.where(chosen, within_all[:, None, :], tiles), axis=2)
    own_tile = jnp.minimum(mine(slot_tile).reshape(-1), tiles - 1)
    slot_tile = slot_tile.reshape(-1)
    row_ids = mod_index * rows_here + jnp.arange(rows_here)
    row_weight = data_weight * (row_ids[None, :] < group_counts[:, None]).astype(F32)
    up = [(i, i + 1) for i in range(copies - 1)]
    down = [(i + 1, i) for i in range(copies - 1)]
    flat_panels = panels.reshape(tx_here, rows_here, foot_len * block_len)
    diagonal = 6.0 + depth_weight.reshape(tiles, block_len)
    share = 1.0 / src_count
    inner = INNER
    across_x = copies // inner
    along_y = [[x * inner + y for y in range(inner)] for x in range(across_x)]
    along_x = [[x * inner + y for x in range(across_x)] for y in range(inner)]

    field = ((tiles, columns, block_len), F32)
    small = ((columns, columns), F32)
    edge = ((plane, columns, block_len), BF16)
    factors = ((columns, columns, 128), F32)
    rim = ((plane, columns, block_len), F32)
    part = ((inner * per, columns, block_len), BF16)

    responses = ((tx_here, columns, rows_here), F32)
    image = pltpu.VMEM((tiles + 1, columns, block_len), F32)
    own_slots = mine(owners_all) * slots + jnp.arange(tx_here)[:, None] * CAP + mine(ranking_all)
    used = jnp.any(
        own_slots.reshape(-1)[:, None] == jnp.arange(copies * slots)[None, :], axis=0
    ).reshape(across_x, inner * slots)
    rank_used = jnp.cumsum(used.astype(jnp.int32), axis=1) - 1
    x_of = owners_all // inner
    filled = jnp.sum(
        (x_of.reshape(src_count, -1)[:, :, None] == jnp.arange(across_x)[None, None, :]).astype(
            jnp.int32
        ),
        axis=1,
    )
    all_slots = inner * slots

    def places(cap):
        at = jnp.sum(
            jnp.where(
                own_slots[:, :, None] == jnp.arange(copies * slots)[None, None, :],
                rank_used.reshape(-1)[None, None, :],
                0,
            ),
            axis=2,
        )
        place = (mine(owners_all) // inner) * (cap + 1) + at
        here = mod_index // inner
        used_here = lax.dynamic_index_in_dim(used, here, 0, keepdims=False)
        rank_here = lax.dynamic_index_in_dim(rank_used, here, 0, keepdims=False)
        slot = jnp.arange(all_slots)
        slot = (slot // slots) * per + slot % slots
        match = used_here[None, :] & (rank_here[None, :] == jnp.arange(cap)[:, None])
        kept = jnp.sum(jnp.where(match, slot[None, :], 0), axis=1)
        kept = jnp.where(jnp.any(match, axis=1), kept, slots)
        return place, kept

    residual = right_side.transpose(1, 2, 0, 3).reshape(field[0])
    sent, first_plane, last_plane = call(
        functools.partial(begin_kernel, inner, slots, plane),
        [part, edge, edge],
        (own_tile, residual),
        (SMEM, VMEM),
    )
    def along(sent, first_plane, last_plane):
        across = lax.all_to_all(sent, "mod", 0, 0, tiled=True, axis_index_groups=along_y)
        before = lax.ppermute(last_plane, "mod", up)
        after = lax.ppermute(first_plane, "mod", down)
        return across, before, after

    def iterations(cap, residual, across, before, after):
        packet = ((across_x * (cap + 1), columns, block_len), BF16)
        place, kept = places(cap)

        def reduced(outgoing):
            halfway = lax.all_to_all(
                outgoing, "mod", 0, 0, tiled=True, axis_index_groups=along_x
            )
            (halfway,) = call(
                functools.partial(widen_kernel, across_x, inner, slots, cap),
                [part],
                (kept, halfway),
                (SMEM, VMEM),
            )
            return lax.all_to_all(halfway, "mod", 0, 0, tiled=True, axis_index_groups=along_y)

        direction = smooth = norm = response = gram_pair = rim_before = rim_after = None
        directions, alphas = [], []
        for iteration in range(ITERS):
            if iteration > 0:
                across, before, after = along(sent, first_plane, last_plane)
            (narrow,) = call(
                functools.partial(narrow_kernel, across_x, inner, slots, cap),
                [packet],
                (kept, across),
                (SMEM, VMEM),
            )
            arrived = lax.all_to_all(
                narrow, "mod", 0, 0, tiled=True, axis_index_groups=along_x
            )
            if iteration == 0:
                smooth, gram_own, rim_before, rim_after = call(
                    functools.partial(regularize_first, plane),
                    [field, small, rim, rim],
                    (residual, before, after, diagonal),
                    (VMEM,) * 4,
                )
                direction = residual
                norm, response, gram_pair, outgoing = call(
                    functools.partial(data_kernel, True, across_x, cap, share),
                    [small, responses, small, packet],
                    (place, arrived, flat_panels, row_weight, gram_own),
                    (SMEM,) + (VMEM,) * 4,
                )
                incoming = reduced(outgoing)
            else:
                gram_own, gram_cross = call(
                    functools.partial(regularize_kernel, plane),
                    [small, small],
                    (residual, before, after, diagonal, smooth),
                    (VMEM,) * 5,
                    scratch=(pltpu.VMEM(field[0], F32),),
                )
                norm, beta, response, gram_pair, outgoing = call(
                    functools.partial(data_kernel, False, across_x, cap, share),
                    [small, factors, responses, small, packet],
                    (place, arrived, flat_panels, row_weight, gram_own, gram_cross,
                     gram_pair, norm, response),
                    (SMEM,) + (VMEM,) * 8,
                )
                incoming = reduced(outgoing)
                direction, smooth, rim_before, rim_after = call(
                    functools.partial(mix_kernel, plane),
                    [field, field, rim, rim],
                    (residual, before, after, diagonal,
                     direction, rim_before,
                     rim_after, beta),
                    (VMEM,) * 8,
                )
            directions.append(direction)
            if iteration + 1 == ITERS:
                (solution,) = call(
                    gather_kernel,
                    [field],
                    (*directions[:-1],
                     *alphas),
                    (VMEM,) * (2 * len(alphas)),
                )
            (handed,) = call(
                functools.partial(sum_kernel, inner, slots),
                [((per, columns, block_len), BF16)],
                (incoming,),
                (VMEM,),
            )
            groups = lax.all_gather(handed, "src", axis=0, tiled=True)
            if iteration + 1 < ITERS:
                residual, alpha, sent, first_plane, last_plane = call(
                    functools.partial(step_kernel, src_count, inner, slots, plane),
                    [field, factors, part, edge, edge],
                    (slot_tile, own_tile, groups, residual, smooth, norm),
                    (SMEM, SMEM) + (VMEM,) * 4,
                    scratch=(image,),
                )
                alphas.append(alpha)
            else:
                residual, solution = call(
                    functools.partial(last_kernel, src_count, slots),
                    [field, field],
                    (slot_tile, groups, residual, smooth, norm, direction,
                     solution),
                    (SMEM,) + (VMEM,) * 6,
                    scratch=(image,),
                )
        return solution, residual

    across, before, after = along(sent, first_plane, last_plane)
    solution, residual = lax.cond(
        jnp.all(filled <= NARROW),
        functools.partial(iterations, NARROW),
        functools.partial(iterations, all_slots),
        residual,
        across,
        before,
        after,
    )

    def to_field(parts):
        return parts.reshape(extent_x, extent_y, columns, block_len).transpose(2, 0, 1, 3)

    return (to_field(solution), to_field(residual))


def solution(mesh):
    placed = (
        P(None, "mod", None, None),
        P("mod", None, None),
        P("src", "mod", None, None),
        P("src", "mod"),
        P(),
        P(),
    )
    return jax.shard_map(
        shards,
        mesh=mesh,
        in_specs=placed,
        out_specs=(P(None, "mod", None, None), P(None, "mod", None, None)),
        check_vma=False,
    )
```

```python
import functools

import jax
import jax.numpy as jnp
from jax import lax
from jax.experimental import pallas as pl
from jax.experimental.pallas import tpu as pltpu
from jax.sharding import PartitionSpec as P

CAP = 2
INNER = 8
NARROW = 48
ITERS = 3
F32 = jnp.float32
BF16 = jnp.bfloat16
VMEM = pl.BlockSpec(memory_space=pltpu.VMEM)
SMEM = pl.BlockSpec(memory_space=pltpu.SMEM)


def call(kernel, outs, args, specs, scratch=(), limit=16 << 20):
    return pl.pallas_call(
        kernel,
        out_shape=[jax.ShapeDtypeStruct(shape, dtype) for shape, dtype in outs],
        in_specs=list(specs),
        out_specs=[VMEM] * len(outs),
        scratch_shapes=list(scratch),
        compiler_params=pltpu.CompilerParams(vmem_limit_bytes=limit),
    )(*args)


def solve_small(system, target):
    size = system.shape[0]
    turned = jnp.concatenate([system, target], axis=0)
    rows = [jnp.broadcast_to(turned[:, i : i + 1], (2 * size, 128)) for i in range(size)]
    for p in range(size):
        base = 8 * ((p + 1) // 8)
        lead = [rows[i][p - (2 * size - rows[i].shape[0])][None, :] for i in range(size)]
        keep = base - (2 * size - rows[0].shape[0])
        pivot = rows[p][keep:] / lead[p]
        rows = [
            pivot if i == p else rows[i][keep:] - lead[i] * pivot for i in range(size)
        ]
    return rows


def matrix_turned(rows):
    lanes = lax.broadcasted_iota(jnp.int32, rows[0].shape, 1)
    total = jnp.zeros(rows[0].shape, F32)
    for i, row in enumerate(rows):
        total = jnp.where(lanes == i, row, total)
    return total[:, : len(rows)]


def split_three(gram):
    size = gram.shape[0]
    high = gram.astype(BF16).astype(F32)
    rest = gram - high
    middle = rest.astype(BF16).astype(F32)
    low = rest - middle
    fill = jnp.zeros((size, 128 - 3 * size), F32)
    return jnp.concatenate([high, middle, low, fill], axis=1).astype(BF16)


def join_three(total):
    size = total.shape[0]
    return total[:, :size] + total[:, size : 2 * size] + total[:, 2 * size : 3 * size]


def read_rows(ref):
    return [ref[i] for i in range(ref.shape[0])]


def mix_tile(tile, spread):
    total = None
    for i, factor in enumerate(spread):
        term = factor * tile[i : i + 1, :]
        total = term if total is None else total + term
    return total


def small_dot(first, second, dims):
    return lax.dot_general(
        first, second, (dims, ((), ())), precision=lax.Precision.HIGHEST, preferred_element_type=F32
    )


def halves(value):
    high = value.astype(BF16)
    return high, (value - high.astype(F32)).astype(BF16)


def nt(first, second):
    return lax.dot_general(first, second, (((1,), (1,)), ((), ())), preferred_element_type=F32)


def gram_halves(first, second):
    (fh, fl), (sh, sl) = first, second
    return nt(fh, sh) + (nt(fh, sl) + nt(fl, sh))


def wide(ref, start, count):
    return jnp.concatenate([ref[start + k] for k in range(count)], axis=1)


def each(count, body, step=8):

    def several(start, carry):
        for k in range(step):
            body(start * step + k)
        return carry

    lax.fori_loop(0, count // step, several, 0)


def gram(first, second, unroll=False):
    step = 8

    def add(k, total):
        one = halves(wide(first, k * step, step))
        two = one if second is first else halves(wide(second, k * step, step))
        return total + gram_halves(one, two)

    start = jnp.zeros((first.shape[1], first.shape[1]), F32)
    return lax.fori_loop(0, first.shape[0] // step, add, start, unroll=unroll)


def pack(residual, own_tile, sent, first_plane, last_plane, copies, slots, plane):
    tiles = residual.shape[0]
    blocks = [residual[own_tile[s]].astype(BF16) for s in range(slots)]
    blocks.append(split_three(gram(residual, residual, unroll=True)))
    for m in range(copies):
        for s in range(slots + 1):
            sent[m * (slots + 1) + s] = blocks[s]
    for y in range(plane):
        first_plane[y] = residual[y].astype(BF16)
        last_plane[y] = residual[tiles - plane + y].astype(BF16)


def begin_kernel(copies, slots, plane, own_tile, residual, sent, first_plane, last_plane):
    pack(residual, own_tile, sent, first_plane, last_plane, copies, slots, plane)


def advance(src_count, slots, slot_tile, groups, residual, smooth, norm, image, fresh):
    tiles = residual.shape[0]
    per = slots + 1
    image[pl.ds(0, tiles)] = smooth[...]

    def add_group(i, curvature):
        for s in range(slots):
            tile = slot_tile[i * slots + s]
            image[tile] = image[tile] + groups[i * per + s].astype(F32)
        return curvature + groups[i * per + slots].astype(F32)

    start = jnp.zeros(groups.shape[1:], F32)
    curvature = join_three(lax.fori_loop(0, src_count, add_group, start))
    spread = solve_small(curvature, norm[...])

    def subtract(l):
        fresh[l] = residual[l] - mix_tile(image[l], spread)

    each(tiles, subtract)
    return spread


def step_kernel(
    src_count, copies, slots, plane, slot_tile, own_tile, groups, residual, smooth, norm,
    fresh, alpha_out, sent, first_plane, last_plane, image,
):
    alpha = advance(src_count, slots, slot_tile, groups, residual, smooth, norm, image, fresh)
    for i, row in enumerate(alpha):
        alpha_out[i] = row
    pack(fresh, own_tile, sent, first_plane, last_plane, copies, slots, plane)


def last_kernel(
    src_count, slots, slot_tile, groups, residual, smooth, norm, direction, solution,
    fresh, solution_out, image,
):
    spread = advance(src_count, slots, slot_tile, groups, residual, smooth, norm, image, fresh)

    def add(l):
        solution_out[l] = solution[l] + mix_tile(direction[l], spread)

    each(residual.shape[0], add)


def smooth_field(field, before, after, diagonal, out, plane):
    tiles = field.shape[0]
    lanes = lax.broadcasted_iota(jnp.int32, field.shape[1:], 1)
    last = field.shape[2] - 1
    end = tiles // plane - 1

    def one_plane(x, carry):
        weights = diagonal[pl.ds(pl.multiple_of(x * plane, plane), plane), :]
        for y in range(plane):
            l = x * plane + y
            tile = field[l]
            beside = jnp.where(lanes == 0, 0.0, pltpu.roll(tile, 1, 1))
            beside = beside + jnp.where(lanes == last, 0.0, pltpu.roll(tile, last, 1))
            if y > 0:
                beside = beside + field[l - 1]
            if y < plane - 1:
                beside = beside + field[l + 1]
            lower = field[jnp.maximum(l - plane, y)]
            upper = field[jnp.minimum(l + plane, end * plane + y)]
            beside = beside + jnp.where(x == 0, before[y].astype(F32), lower)
            beside = beside + jnp.where(x == end, after[y].astype(F32), upper)
            out[l] = weights[y : y + 1, :] * tile - beside
        return carry

    lax.fori_loop(0, end + 1, one_plane, 0)


def regularize_first(plane, field, before, after, diagonal, smooth, gram_own, rim_before, rim_after):
    rim_before[...] = before[...].astype(F32)
    rim_after[...] = after[...].astype(F32)
    smooth_field(field, before, after, diagonal, smooth, plane)
    gram_own[...] = gram(field, smooth)


def regularize_kernel(
    plane, field, before, after, diagonal, smooth_old, gram_own, gram_cross, fresh
):
    gram_cross[...] = gram(field, smooth_old)
    smooth_field(field, before, after, diagonal, fresh, plane)
    gram_own[...] = gram(field, fresh)


def data_kernel(first, across_x, cap, share, place, arrived, panels, row_weight, *refs):
    if first:
        gram_own, norm_out, response_out, gram_out, outgoing = refs
    else:
        (gram_own, gram_cross, gram_old, norm_old, response_old,
         norm_out, beta_out, response_out, gram_out, outgoing) = refs
    per = cap + 1
    tx_here, rows_here, width = panels.shape
    columns, block_len = arrived.shape[1:]
    foot_len = width // block_len
    total = arrived[cap].astype(F32)
    for x in range(1, across_x):
        total = total + arrived[x * per + cap].astype(F32)
    norm = join_three(total)
    norm_out[...] = norm
    beta = None
    pair = gram_own[...]
    if not first:
        rows = solve_small(norm_old[...], norm)
        for i, row in enumerate(rows):
            beta_out[i] = row
        beta = matrix_turned(rows)
        cross = small_dot(beta, gram_cross[...], ((1,), (1,)))
        inner = small_dot(beta, gram_old[...], ((1,), (0,)))
        pair = pair + cross + cross.T + small_dot(inner, beta, ((1,), (1,)))
    gram_out[...] = pair
    curvature = share * pair
    empty = jnp.zeros((columns, block_len), BF16)
    responses, weights = [], []
    for x in range(across_x):
        for s in range(cap):
            outgoing[x * per + s] = empty
    for t in range(tx_here):
        picked = jnp.concatenate([arrived[place[t, f]] for f in range(foot_len)], axis=1)
        response = nt(picked, panels[t])
        if not first:
            response = response + small_dot(beta, response_old[t], ((1,), (0,)))
        response_out[t] = response
        weighted = response * row_weight[t : t + 1, :]
        responses.append(response)
        weights.append(weighted)
    for t in range(tx_here):
        shares = jnp.dot(
            weights[t].astype(BF16), panels[t], preferred_element_type=F32
        ).astype(BF16)
        for f in range(foot_len):
            outgoing[place[t, f]] = shares[:, f * block_len : (f + 1) * block_len]
    curvature = curvature + gram_halves(
        halves(jnp.concatenate(responses, axis=1)), halves(jnp.concatenate(weights, axis=1))
    )
    pieces = split_three(curvature)
    for x in range(across_x):
        outgoing[x * per + cap] = pieces


def mix_kernel(
    plane, fresh, before, after, diagonal, direction, rim_before, rim_after, beta,
    direction_out, smooth_out, rim_before_out, rim_after_out,
):
    spread = read_rows(beta)

    def inside(l):
        direction_out[l] = fresh[l] + mix_tile(direction[l], spread)

    def beside(y):
        rim_before_out[y] = before[y].astype(F32) + mix_tile(rim_before[y], spread)
        rim_after_out[y] = after[y].astype(F32) + mix_tile(rim_after[y], spread)

    each(fresh.shape[0], inside)
    each(plane, beside, 4)
    smooth_field(direction_out, rim_before_out, rim_after_out, diagonal, smooth_out, plane)


def gather_kernel(*refs):
    count = (len(refs) - 1) // 2
    directions, alphas, out = refs[:count], refs[count : 2 * count], refs[-1]
    spreads = [read_rows(alpha) for alpha in alphas]
    for k in range(count):

        def add(l):
            term = mix_tile(directions[k][l], spreads[k])
            out[l] = term if k == 0 else out[l] + term

        each(out.shape[0], add)


def narrow_kernel(across_x, inner, slots, cap, kept, across, out):
    per = slots + 1
    total = across[slots].astype(F32)
    for y in range(1, inner):
        total = total + across[y * per + slots].astype(F32)
    pieces = split_three(join_three(total))
    for x in range(across_x):
        out[x * (cap + 1) + cap] = pieces
    for d in range(cap):
        block = across[kept[d]]
        for x in range(across_x):
            out[x * (cap + 1) + d] = block


def widen_kernel(across_x, inner, slots, cap, kept, incoming, out):
    per = slots + 1
    empty = jnp.zeros(out.shape[1:], BF16)
    for s in range(inner * per):
        out[s] = empty

    def summed(d):
        total = incoming[d].astype(F32)
        for x in range(1, across_x):
            total = total + incoming[x * (cap + 1) + d].astype(F32)
        return total

    for d in range(cap):
        out[kept[d]] = summed(d).astype(BF16)
    pieces = split_three(join_three(summed(cap)))
    for y in range(inner):
        out[y * per + slots] = pieces


def sum_kernel(copies, slots, incoming, handed):
    per = slots + 1
    for s in range(per):
        total = incoming[s].astype(F32)
        for m in range(1, copies):
            total = total + incoming[m * per + s].astype(F32)
        handed[s] = total.astype(BF16) if s < slots else split_three(join_three(total))


def owners_ranks(tile_ids, blocks_dev):
    owners = tile_ids // blocks_dev
    position = jnp.arange(tile_ids.shape[1])
    before = (owners[:, :, None] == owners[:, None, :]) & (
        position[None, None, :] < position[None, :, None]
    )
    ranking = jnp.sum(before.astype(jnp.int32), axis=2)
    return (owners, tile_ids - owners * blocks_dev, ranking)


def shards(right_side, depth_weight, panels, data_weight, footprints, counts):
    columns, extent_x, extent_y, block_len = right_side.shape
    tx_here, rows_here, foot_len, _ = panels.shape
    copies = lax.axis_size("mod")
    src_count = lax.axis_size("src")
    tiles = extent_x * extent_y
    plane = extent_y
    slots = tx_here * CAP
    per = slots + 1
    mod_index = lax.axis_index("mod")
    src_index = lax.axis_index("src")
    group_counts = lax.dynamic_slice_in_dim(counts, src_index * tx_here, tx_here, 0)
    owners_all, within_all, ranking_all = owners_ranks(footprints, tiles)
    mine = lambda ids: lax.dynamic_slice_in_dim(ids, src_index * tx_here, tx_here, 0)
    chosen = (owners_all == mod_index)[:, None, :] & (
        ranking_all[:, None, :] == jnp.arange(CAP)[None, :, None]
    )
    slot_tile = jnp.min(jnp.where(chosen, within_all[:, None, :], tiles), axis=2)
    own_tile = jnp.minimum(mine(slot_tile).reshape(-1), tiles - 1)
    slot_tile = slot_tile.reshape(-1)
    row_ids = mod_index * rows_here + jnp.arange(rows_here)
    row_weight = data_weight * (row_ids[None, :] < group_counts[:, None]).astype(F32)
    up = [(i, i + 1) for i in range(copies - 1)]
    down = [(i + 1, i) for i in range(copies - 1)]
    flat_panels = panels.reshape(tx_here, rows_here, foot_len * block_len)
    diagonal = 6.0 + depth_weight.reshape(tiles, block_len)
    share = 1.0 / src_count
    inner = INNER
    across_x = copies // inner
    along_y = [[x * inner + y for y in range(inner)] for x in range(across_x)]
    along_x = [[x * inner + y for x in range(across_x)] for y in range(inner)]

    field = ((tiles, columns, block_len), F32)
    small = ((columns, columns), F32)
    edge = ((plane, columns, block_len), BF16)
    factors = ((columns, columns, 128), F32)
    rim = ((plane, columns, block_len), F32)
    part = ((inner * per, columns, block_len), BF16)

    responses = ((tx_here, columns, rows_here), F32)
    image = pltpu.VMEM((tiles + 1, columns, block_len), F32)
    own_slots = mine(owners_all) * slots + jnp.arange(tx_here)[:, None] * CAP + mine(ranking_all)
    used = jnp.any(
        own_slots.reshape(-1)[:, None] == jnp.arange(copies * slots)[None, :], axis=0
    ).reshape(across_x, inner * slots)
    rank_used = jnp.cumsum(used.astype(jnp.int32), axis=1) - 1
    x_of = owners_all // inner
    filled = jnp.sum(
        (x_of.reshape(src_count, -1)[:, :, None] == jnp.arange(across_x)[None, None, :]).astype(
            jnp.int32
        ),
        axis=1,
    )
    all_slots = inner * slots

    def places(cap):
        at = jnp.sum(
            jnp.where(
                own_slots[:, :, None] == jnp.arange(copies * slots)[None, None, :],
                rank_used.reshape(-1)[None, None, :],
                0,
            ),
            axis=2,
        )
        place = (mine(owners_all) // inner) * (cap + 1) + at
        here = mod_index // inner
        used_here = lax.dynamic_index_in_dim(used, here, 0, keepdims=False)
        rank_here = lax.dynamic_index_in_dim(rank_used, here, 0, keepdims=False)
        slot = jnp.arange(all_slots)
        slot = (slot // slots) * per + slot % slots
        match = used_here[None, :] & (rank_here[None, :] == jnp.arange(cap)[:, None])
        kept = jnp.sum(jnp.where(match, slot[None, :], 0), axis=1)
        kept = jnp.where(jnp.any(match, axis=1), kept, slots)
        return place, kept

    residual = right_side.transpose(1, 2, 0, 3).reshape(field[0])
    sent, first_plane, last_plane = call(
        functools.partial(begin_kernel, inner, slots, plane),
        [part, edge, edge],
        (own_tile, residual),
        (SMEM, VMEM),
    )
    def along(sent, first_plane, last_plane):
        across = lax.all_to_all(sent, "mod", 0, 0, tiled=True, axis_index_groups=along_y)
        before = lax.ppermute(last_plane, "mod", up)
        after = lax.ppermute(first_plane, "mod", down)
        return across, before, after

    def iterations(cap, residual, across, before, after):
        packet = ((across_x * (cap + 1), columns, block_len), BF16)
        place, kept = places(cap)

        def reduced(outgoing):
            halfway = lax.all_to_all(
                outgoing, "mod", 0, 0, tiled=True, axis_index_groups=along_x
            )
            (halfway,) = call(
                functools.partial(widen_kernel, across_x, inner, slots, cap),
                [part],
                (kept, halfway),
                (SMEM, VMEM),
            )
            return lax.all_to_all(halfway, "mod", 0, 0, tiled=True, axis_index_groups=along_y)

        direction = smooth = norm = response = gram_pair = rim_before = rim_after = None
        directions, alphas = [], []
        for iteration in range(ITERS):
            if iteration > 0:
                across, before, after = along(sent, first_plane, last_plane)
            (narrow,) = call(
                functools.partial(narrow_kernel, across_x, inner, slots, cap),
                [packet],
                (kept, across),
                (SMEM, VMEM),
            )
            arrived = lax.all_to_all(
                narrow, "mod", 0, 0, tiled=True, axis_index_groups=along_x
            )
            if iteration == 0:
                smooth, gram_own, rim_before, rim_after = call(
                    functools.partial(regularize_first, plane),
                    [field, small, rim, rim],
                    (residual, before, after, diagonal),
                    (VMEM,) * 4,
                )
                direction = residual
                norm, response, gram_pair, outgoing = call(
                    functools.partial(data_kernel, True, across_x, cap, share),
                    [small, responses, small, packet],
                    (place, arrived, flat_panels, row_weight, gram_own),
                    (SMEM,) + (VMEM,) * 4,
                )
                incoming = reduced(outgoing)
            else:
                gram_own, gram_cross = call(
                    functools.partial(regularize_kernel, plane),
                    [small, small],
                    (residual, before, after, diagonal, smooth),
                    (VMEM,) * 5,
                    scratch=(pltpu.VMEM(field[0], F32),),
                )
                norm, beta, response, gram_pair, outgoing = call(
                    functools.partial(data_kernel, False, across_x, cap, share),
                    [small, factors, responses, small, packet],
                    (place, arrived, flat_panels, row_weight, gram_own, gram_cross,
                     gram_pair, norm, response),
                    (SMEM,) + (VMEM,) * 8,
                )
                incoming = reduced(outgoing)
                direction, smooth, rim_before, rim_after = call(
                    functools.partial(mix_kernel, plane),
                    [field, field, rim, rim],
                    (residual, before, after, diagonal,
                     direction, rim_before,
                     rim_after, beta),
                    (VMEM,) * 8,
                )
            directions.append(direction)
            if iteration + 1 == ITERS:
                (solution,) = call(
                    gather_kernel,
                    [field],
                    (*directions[:-1],
                     *alphas),
                    (VMEM,) * (2 * len(alphas)),
                )
            (handed,) = call(
                functools.partial(sum_kernel, inner, slots),
                [((per, columns, block_len), BF16)],
                (incoming,),
                (VMEM,),
            )
            groups = lax.all_gather(handed, "src", axis=0, tiled=True)
            if iteration + 1 < ITERS:
                residual, alpha, sent, first_plane, last_plane = call(
                    functools.partial(step_kernel, src_count, inner, slots, plane),
                    [field, factors, part, edge, edge],
                    (slot_tile, own_tile, groups, residual, smooth, norm),
                    (SMEM, SMEM) + (VMEM,) * 4,
                    scratch=(image,),
                )
                alphas.append(alpha)
            else:
                residual, solution = call(
                    functools.partial(last_kernel, src_count, slots),
                    [field, field],
                    (slot_tile, groups, residual, smooth, norm, direction,
                     solution),
                    (SMEM,) + (VMEM,) * 6,
                    scratch=(image,),
                )
        return solution, residual

    across, before, after = along(sent, first_plane, last_plane)
    solution, residual = lax.cond(
        jnp.all(filled <= NARROW),
        functools.partial(iterations, NARROW),
        functools.partial(iterations, all_slots),
        residual,
        across,
        before,
        after,
    )

    def to_field(parts):
        return parts.reshape(extent_x, extent_y, columns, block_len).transpose(2, 0, 1, 3)

    return (to_field(solution), to_field(residual))


def solution(mesh):
    placed = (
        P(None, "mod", None, None),
        P("mod", None, None),
        P("src", "mod", None, None),
        P("src", "mod"),
        P(),
        P(),
    )
    return jax.shard_map(
        shards,
        mesh=mesh,
        in_specs=placed,
        out_specs=(P(None, "mod", None, None), P(None, "mod", None, None)),
        check_vma=False,
    )
```

```python
import functools

import jax
import jax.numpy as jnp
from jax import lax
from jax.experimental import pallas as pl
from jax.experimental.pallas import tpu as pltpu
from jax.sharding import PartitionSpec as P

CAP = 2
INNER = 8
NARROW = 46
ITERS = 3
F32 = jnp.float32
BF16 = jnp.bfloat16
VMEM = pl.BlockSpec(memory_space=pltpu.VMEM)
SMEM = pl.BlockSpec(memory_space=pltpu.SMEM)


def call(kernel, outs, args, specs, scratch=(), limit=16 << 20):
    return pl.pallas_call(
        kernel,
        out_shape=[jax.ShapeDtypeStruct(shape, dtype) for shape, dtype in outs],
        in_specs=list(specs),
        out_specs=[VMEM] * len(outs),
        scratch_shapes=list(scratch),
        compiler_params=pltpu.CompilerParams(vmem_limit_bytes=limit),
    )(*args)


def solve_small(system, target):
    size = system.shape[0]
    turned = jnp.concatenate([system, target], axis=0)
    rows = [jnp.broadcast_to(turned[:, i : i + 1], (2 * size, 128)) for i in range(size)]
    for p in range(size):
        base = 8 * ((p + 1) // 8)
        lead = [rows[i][p - (2 * size - rows[i].shape[0])][None, :] for i in range(size)]
        keep = base - (2 * size - rows[0].shape[0])
        pivot = rows[p][keep:] / lead[p]
        rows = [
            pivot if i == p else rows[i][keep:] - lead[i] * pivot for i in range(size)
        ]
    return rows


def matrix_turned(rows):
    lanes = lax.broadcasted_iota(jnp.int32, rows[0].shape, 1)
    total = jnp.zeros(rows[0].shape, F32)
    for i, row in enumerate(rows):
        total = jnp.where(lanes == i, row, total)
    return total[:, : len(rows)]


def split_three(gram):
    size = gram.shape[0]
    high = gram.astype(BF16).astype(F32)
    rest = gram - high
    middle = rest.astype(BF16).astype(F32)
    low = rest - middle
    fill = jnp.zeros((size, 128 - 3 * size), F32)
    return jnp.concatenate([high, middle, low, fill], axis=1).astype(BF16)


def join_three(total):
    size = total.shape[0]
    return total[:, :size] + total[:, size : 2 * size] + total[:, 2 * size : 3 * size]


def read_rows(ref):
    return [ref[i] for i in range(ref.shape[0])]


def mix_tile(tile, spread):
    total = None
    for i, factor in enumerate(spread):
        term = factor * tile[i : i + 1, :]
        total = term if total is None else total + term
    return total


def small_dot(first, second, dims):
    return lax.dot_general(
        first, second, (dims, ((), ())), precision=lax.Precision.HIGHEST, preferred_element_type=F32
    )


def halves(value):
    high = value.astype(BF16)
    return high, (value - high.astype(F32)).astype(BF16)


def nt(first, second):
    return lax.dot_general(first, second, (((1,), (1,)), ((), ())), preferred_element_type=F32)


def gram_halves(first, second):
    (fh, fl), (sh, sl) = first, second
    return nt(fh, sh) + (nt(fh, sl) + nt(fl, sh))


def wide(ref, start, count):
    return jnp.concatenate([ref[start + k] for k in range(count)], axis=1)


def each(count, body, step=8):

    def several(start, carry):
        for k in range(step):
            body(start * step + k)
        return carry

    lax.fori_loop(0, count // step, several, 0)


def gram(first, second, unroll=False):
    step = 8

    def add(k, total):
        one = halves(wide(first, k * step, step))
        two = one if second is first else halves(wide(second, k * step, step))
        return total + gram_halves(one, two)

    start = jnp.zeros((first.shape[1], first.shape[1]), F32)
    return lax.fori_loop(0, first.shape[0] // step, add, start, unroll=unroll)


def pack(residual, own_tile, sent, first_plane, last_plane, copies, slots, plane):
    tiles = residual.shape[0]
    blocks = [residual[own_tile[s]].astype(BF16) for s in range(slots)]
    blocks.append(split_three(gram(residual, residual, unroll=True)))
    for m in range(copies):
        for s in range(slots + 1):
            sent[m * (slots + 1) + s] = blocks[s]
    for y in range(plane):
        first_plane[y] = residual[y].astype(BF16)
        last_plane[y] = residual[tiles - plane + y].astype(BF16)


def begin_kernel(copies, slots, plane, own_tile, residual, sent, first_plane, last_plane):
    pack(residual, own_tile, sent, first_plane, last_plane, copies, slots, plane)


def advance(src_count, slots, slot_tile, groups, residual, smooth, norm, image, fresh):
    tiles = residual.shape[0]
    per = slots + 1
    image[pl.ds(0, tiles)] = smooth[...]

    def add_group(i, curvature):
        for s in range(slots):
            tile = slot_tile[i * slots + s]
            image[tile] = image[tile] + groups[i * per + s].astype(F32)
        return curvature + groups[i * per + slots].astype(F32)

    start = jnp.zeros(groups.shape[1:], F32)
    curvature = join_three(lax.fori_loop(0, src_count, add_group, start))
    spread = solve_small(curvature, norm[...])

    def subtract(l):
        fresh[l] = residual[l] - mix_tile(image[l], spread)

    each(tiles, subtract)
    return spread


def step_kernel(
    src_count, copies, slots, plane, slot_tile, own_tile, groups, residual, smooth, norm,
    fresh, alpha_out, sent, first_plane, last_plane, image,
):
    alpha = advance(src_count, slots, slot_tile, groups, residual, smooth, norm, image, fresh)
    for i, row in enumerate(alpha):
        alpha_out[i] = row
    pack(fresh, own_tile, sent, first_plane, last_plane, copies, slots, plane)


def last_kernel(
    src_count, slots, slot_tile, groups, residual, smooth, norm, direction, solution,
    fresh, solution_out, image,
):
    spread = advance(src_count, slots, slot_tile, groups, residual, smooth, norm, image, fresh)

    def add(l):
        solution_out[l] = solution[l] + mix_tile(direction[l], spread)

    each(residual.shape[0], add)


def smooth_field(field, before, after, diagonal, out, plane):
    tiles = field.shape[0]
    lanes = lax.broadcasted_iota(jnp.int32, field.shape[1:], 1)
    last = field.shape[2] - 1
    end = tiles // plane - 1

    def one_plane(x, carry):
        weights = diagonal[pl.ds(pl.multiple_of(x * plane, plane), plane), :]
        for y in range(plane):
            l = x * plane + y
            tile = field[l]
            beside = jnp.where(lanes == 0, 0.0, pltpu.roll(tile, 1, 1))
            beside = beside + jnp.where(lanes == last, 0.0, pltpu.roll(tile, last, 1))
            if y > 0:
                beside = beside + field[l - 1]
            if y < plane - 1:
                beside = beside + field[l + 1]
            lower = field[jnp.maximum(l - plane, y)]
            upper = field[jnp.minimum(l + plane, end * plane + y)]
            beside = beside + jnp.where(x == 0, before[y].astype(F32), lower)
            beside = beside + jnp.where(x == end, after[y].astype(F32), upper)
            out[l] = weights[y : y + 1, :] * tile - beside
        return carry

    lax.fori_loop(0, end + 1, one_plane, 0)


def regularize_first(plane, field, before, after, diagonal, smooth, gram_own, rim_before, rim_after):
    rim_before[...] = before[...].astype(F32)
    rim_after[...] = after[...].astype(F32)
    smooth_field(field, before, after, diagonal, smooth, plane)
    gram_own[...] = gram(field, smooth)


def regularize_kernel(
    plane, field, before, after, diagonal, smooth_old, gram_own, gram_cross, fresh
):
    gram_cross[...] = gram(field, smooth_old)
    smooth_field(field, before, after, diagonal, fresh, plane)
    gram_own[...] = gram(field, fresh)


def data_kernel(first, across_x, cap, share, place, arrived, panels, row_weight, *refs):
    if first:
        gram_own, norm_out, response_out, gram_out, outgoing = refs
    else:
        (gram_own, gram_cross, gram_old, norm_old, response_old,
         norm_out, beta_out, response_out, gram_out, outgoing) = refs
    per = cap + 1
    tx_here, rows_here, width = panels.shape
    columns, block_len = arrived.shape[1:]
    foot_len = width // block_len
    total = arrived[cap].astype(F32)
    for x in range(1, across_x):
        total = total + arrived[x * per + cap].astype(F32)
    norm = join_three(total)
    norm_out[...] = norm
    beta = None
    pair = gram_own[...]
    if not first:
        rows = solve_small(norm_old[...], norm)
        for i, row in enumerate(rows):
            beta_out[i] = row
        beta = matrix_turned(rows)
        cross = small_dot(beta, gram_cross[...], ((1,), (1,)))
        inner = small_dot(beta, gram_old[...], ((1,), (0,)))
        pair = pair + cross + cross.T + small_dot(inner, beta, ((1,), (1,)))
    gram_out[...] = pair
    curvature = share * pair
    empty = jnp.zeros((columns, block_len), BF16)
    responses, weights = [], []
    for x in range(across_x):
        for s in range(cap):
            outgoing[x * per + s] = empty
    for t in range(tx_here):
        picked = jnp.concatenate([arrived[place[t, f]] for f in range(foot_len)], axis=1)
        response = nt(picked, panels[t])
        if not first:
            response = response + small_dot(beta, response_old[t], ((1,), (0,)))
        response_out[t] = response
        weighted = response * row_weight[t : t + 1, :]
        responses.append(response)
        weights.append(weighted)
    for t in range(tx_here):
        shares = jnp.dot(
            weights[t].astype(BF16), panels[t], preferred_element_type=F32
        ).astype(BF16)
        for f in range(foot_len):
            outgoing[place[t, f]] = shares[:, f * block_len : (f + 1) * block_len]
    curvature = curvature + gram_halves(
        halves(jnp.concatenate(responses, axis=1)), halves(jnp.concatenate(weights, axis=1))
    )
    pieces = split_three(curvature)
    for x in range(across_x):
        outgoing[x * per + cap] = pieces


def mix_kernel(
    plane, fresh, before, after, diagonal, direction, rim_before, rim_after, beta,
    direction_out, smooth_out, rim_before_out, rim_after_out,
):
    spread = read_rows(beta)

    def inside(l):
        direction_out[l] = fresh[l] + mix_tile(direction[l], spread)

    def beside(y):
        rim_before_out[y] = before[y].astype(F32) + mix_tile(rim_before[y], spread)
        rim_after_out[y] = after[y].astype(F32) + mix_tile(rim_after[y], spread)

    each(fresh.shape[0], inside)
    each(plane, beside, 4)
    smooth_field(direction_out, rim_before_out, rim_after_out, diagonal, smooth_out, plane)


def gather_kernel(*refs):
    count = (len(refs) - 1) // 2
    directions, alphas, out = refs[:count], refs[count : 2 * count], refs[-1]
    spreads = [read_rows(alpha) for alpha in alphas]
    for k in range(count):

        def add(l):
            term = mix_tile(directions[k][l], spreads[k])
            out[l] = term if k == 0 else out[l] + term

        each(out.shape[0], add)


def narrow_kernel(across_x, inner, slots, cap, kept, across, out):
    per = slots + 1
    total = across[slots].astype(F32)
    for y in range(1, inner):
        total = total + across[y * per + slots].astype(F32)
    pieces = split_three(join_three(total))
    for x in range(across_x):
        out[x * (cap + 1) + cap] = pieces
    for d in range(cap):
        block = across[kept[d]]
        for x in range(across_x):
            out[x * (cap + 1) + d] = block


def widen_kernel(across_x, inner, slots, cap, kept, incoming, out):
    per = slots + 1
    empty = jnp.zeros(out.shape[1:], BF16)
    for s in range(inner * per):
        out[s] = empty

    def summed(d):
        total = incoming[d].astype(F32)
        for x in range(1, across_x):
            total = total + incoming[x * (cap + 1) + d].astype(F32)
        return total

    for d in range(cap):
        out[kept[d]] = summed(d).astype(BF16)
    pieces = split_three(join_three(summed(cap)))
    for y in range(inner):
        out[y * per + slots] = pieces


def sum_kernel(copies, slots, incoming, handed):
    per = slots + 1
    for s in range(per):
        total = incoming[s].astype(F32)
        for m in range(1, copies):
            total = total + incoming[m * per + s].astype(F32)
        handed[s] = total.astype(BF16) if s < slots else split_three(join_three(total))


def owners_ranks(tile_ids, blocks_dev):
    owners = tile_ids // blocks_dev
    position = jnp.arange(tile_ids.shape[1])
    before = (owners[:, :, None] == owners[:, None, :]) & (
        position[None, None, :] < position[None, :, None]
    )
    ranking = jnp.sum(before.astype(jnp.int32), axis=2)
    return (owners, tile_ids - owners * blocks_dev, ranking)


def shards(right_side, depth_weight, panels, data_weight, footprints, counts):
    columns, extent_x, extent_y, block_len = right_side.shape
    tx_here, rows_here, foot_len, _ = panels.shape
    copies = lax.axis_size("mod")
    src_count = lax.axis_size("src")
    tiles = extent_x * extent_y
    plane = extent_y
    slots = tx_here * CAP
    per = slots + 1
    mod_index = lax.axis_index("mod")
    src_index = lax.axis_index("src")
    group_counts = lax.dynamic_slice_in_dim(counts, src_index * tx_here, tx_here, 0)
    group = lax.dynamic_slice_in_dim(footprints, src_index * tx_here, tx_here, 0)
    owners, _, ranking = owners_ranks(group, tiles)

    def tiles_of_slots(tile_ids):
        its_owners, within, its_ranking = owners_ranks(tile_ids, tiles)
        chosen = (its_owners == mod_index)[:, None, :] & (
            its_ranking[:, None, :] == jnp.arange(CAP)[None, :, None]
        )
        return jnp.min(jnp.where(chosen, within[:, None, :], tiles), axis=2).reshape(-1)

    own_tile = jnp.minimum(tiles_of_slots(group), tiles - 1)
    row_ids = mod_index * rows_here + jnp.arange(rows_here)
    row_weight = data_weight * (row_ids[None, :] < group_counts[:, None]).astype(F32)
    up = [(i, i + 1) for i in range(copies - 1)]
    down = [(i + 1, i) for i in range(copies - 1)]
    flat_panels = lax.optimization_barrier(
        panels.reshape(tx_here, rows_here, foot_len * block_len)
    )
    diagonal = 6.0 + depth_weight.reshape(tiles, block_len)
    share = 1.0 / src_count
    inner = INNER
    across_x = copies // inner
    along_y = [[x * inner + y for y in range(inner)] for x in range(across_x)]
    along_x = [[x * inner + y for x in range(across_x)] for y in range(inner)]

    field = ((tiles, columns, block_len), F32)
    small = ((columns, columns), F32)
    edge = ((plane, columns, block_len), BF16)
    factors = ((columns, columns, 128), F32)
    rim = ((plane, columns, block_len), F32)
    part = ((inner * per, columns, block_len), BF16)

    responses = ((tx_here, columns, rows_here), F32)
    image = pltpu.VMEM((tiles + 1, columns, block_len), F32)
    own_slots = owners * slots + jnp.arange(tx_here)[:, None] * CAP + ranking
    used = jnp.any(
        own_slots.reshape(-1)[:, None] == jnp.arange(copies * slots)[None, :], axis=0
    ).reshape(across_x, inner * slots)
    rank_used = jnp.cumsum(used.astype(jnp.int32), axis=1) - 1
    x_of = footprints // (tiles * inner)
    filled = jnp.sum(
        (x_of.reshape(src_count, -1)[:, :, None] == jnp.arange(across_x)[None, None, :]).astype(
            jnp.int32
        ),
        axis=1,
    )
    all_slots = inner * slots

    def places(cap):
        at = jnp.sum(
            jnp.where(
                own_slots[:, :, None] == jnp.arange(copies * slots)[None, None, :],
                rank_used.reshape(-1)[None, None, :],
                0,
            ),
            axis=2,
        )
        place = (owners // inner) * (cap + 1) + at
        here = mod_index // inner
        used_here = lax.dynamic_index_in_dim(used, here, 0, keepdims=False)
        rank_here = lax.dynamic_index_in_dim(rank_used, here, 0, keepdims=False)
        slot = jnp.arange(all_slots)
        slot = (slot // slots) * per + slot % slots
        match = used_here[None, :] & (rank_here[None, :] == jnp.arange(cap)[:, None])
        kept = jnp.sum(jnp.where(match, slot[None, :], 0), axis=1)
        kept = jnp.where(jnp.any(match, axis=1), kept, slots)
        return place, kept

    residual = right_side.transpose(1, 2, 0, 3).reshape(field[0])
    sent, first_plane, last_plane = call(
        functools.partial(begin_kernel, inner, slots, plane),
        [part, edge, edge],
        (own_tile, residual),
        (SMEM, VMEM),
    )
    def to_field(parts):
        return parts.reshape(extent_x, extent_y, columns, block_len).transpose(2, 0, 1, 3)

    def along(sent, first_plane, last_plane):
        across = lax.all_to_all(sent, "mod", 0, 0, tiled=True, axis_index_groups=along_y)
        before = lax.ppermute(last_plane, "mod", up)
        after = lax.ppermute(first_plane, "mod", down)
        return across, before, after

    def iterations(cap, residual, across, before, after):
        packet = ((across_x * (cap + 1), columns, block_len), BF16)
        place, kept = places(cap)
        place, slot_tile = lax.optimization_barrier((place, tiles_of_slots(footprints)))

        def reduced(outgoing):
            halfway = lax.all_to_all(
                outgoing, "mod", 0, 0, tiled=True, axis_index_groups=along_x
            )
            (halfway,) = call(
                functools.partial(widen_kernel, across_x, inner, slots, cap),
                [part],
                (kept, halfway),
                (SMEM, VMEM),
            )
            return lax.all_to_all(halfway, "mod", 0, 0, tiled=True, axis_index_groups=along_y)

        direction = smooth = norm = response = gram_pair = rim_before = rim_after = None
        directions, alphas = [], []
        for iteration in range(ITERS):
            if iteration > 0:
                across, before, after = along(sent, first_plane, last_plane)
            (narrow,) = call(
                functools.partial(narrow_kernel, across_x, inner, slots, cap),
                [packet],
                (kept, across),
                (SMEM, VMEM),
            )
            arrived = lax.all_to_all(
                narrow, "mod", 0, 0, tiled=True, axis_index_groups=along_x
            )
            if iteration == 0:
                smooth, gram_own, rim_before, rim_after = call(
                    functools.partial(regularize_first, plane),
                    [field, small, rim, rim],
                    (residual, before, after, diagonal),
                    (VMEM,) * 4,
                )
                direction = residual
                norm, response, gram_pair, outgoing = call(
                    functools.partial(data_kernel, True, across_x, cap, share),
                    [small, responses, small, packet],
                    (place, arrived, flat_panels, row_weight, gram_own),
                    (SMEM,) + (VMEM,) * 4,
                )
                incoming = reduced(outgoing)
            else:
                gram_own, gram_cross = call(
                    functools.partial(regularize_kernel, plane),
                    [small, small],
                    (residual, before, after, diagonal, smooth),
                    (VMEM,) * 5,
                    scratch=(pltpu.VMEM(field[0], F32),),
                )
                norm, beta, response, gram_pair, outgoing = call(
                    functools.partial(data_kernel, False, across_x, cap, share),
                    [small, factors, responses, small, packet],
                    (place, arrived, flat_panels, row_weight, gram_own, gram_cross,
                     gram_pair, norm, response),
                    (SMEM,) + (VMEM,) * 8,
                )
                incoming = reduced(outgoing)
                direction, smooth, rim_before, rim_after = call(
                    functools.partial(mix_kernel, plane),
                    [field, field, rim, rim],
                    (residual, before, after, diagonal,
                     direction, rim_before,
                     rim_after, beta),
                    (VMEM,) * 8,
                )
            directions.append(direction)
            if iteration + 1 == ITERS:
                (solution,) = call(
                    gather_kernel,
                    [field],
                    (*directions[:-1],
                     *alphas),
                    (VMEM,) * (2 * len(alphas)),
                )
            (handed,) = call(
                functools.partial(sum_kernel, inner, slots),
                [((per, columns, block_len), BF16)],
                (incoming,),
                (VMEM,),
            )
            groups = lax.all_gather(handed, "src", axis=0, tiled=True)
            if iteration + 1 < ITERS:
                residual, alpha, sent, first_plane, last_plane = call(
                    functools.partial(step_kernel, src_count, inner, slots, plane),
                    [field, factors, part, edge, edge],
                    (slot_tile, own_tile, groups, residual, smooth, norm),
                    (SMEM, SMEM) + (VMEM,) * 4,
                    scratch=(image,),
                )
                alphas.append(alpha)
            else:
                residual, solution = call(
                    functools.partial(last_kernel, src_count, slots),
                    [field, field],
                    (slot_tile, groups, residual, smooth, norm, direction,
                     solution),
                    (SMEM,) + (VMEM,) * 6,
                    scratch=(image,),
                )
        return to_field(solution), to_field(residual)

    across, before, after = along(sent, first_plane, last_plane)
    solution, residual = lax.cond(
        jnp.all(filled <= NARROW),
        functools.partial(iterations, NARROW),
        functools.partial(iterations, all_slots),
        residual,
        across,
        before,
        after,
    )

    return solution, residual


def solution(mesh):
    placed = (
        P(None, "mod", None, None),
        P("mod", None, None),
        P("src", "mod", None, None),
        P("src", "mod"),
        P(),
        P(),
    )
    return jax.shard_map(
        shards,
        mesh=mesh,
        in_specs=placed,
        out_specs=(P(None, "mod", None, None), P(None, "mod", None, None)),
        check_vma=False,
    )
```

```python
import functools

import jax
import jax.numpy as jnp
from jax import lax
from jax.experimental import pallas as pl
from jax.experimental.pallas import tpu as pltpu
from jax.sharding import PartitionSpec as P

CAP = 2
INNER = 8
NARROW = 46
ITERS = 3
F32 = jnp.float32
BF16 = jnp.bfloat16
VMEM = pl.BlockSpec(memory_space=pltpu.VMEM)
SMEM = pl.BlockSpec(memory_space=pltpu.SMEM)
ANY = pl.BlockSpec(memory_space=pl.ANY)


def call(kernel, outs, args, specs, scratch=(), limit=16 << 20):
    return pl.pallas_call(
        kernel,
        out_shape=[jax.ShapeDtypeStruct(shape, dtype) for shape, dtype in outs],
        in_specs=list(specs),
        out_specs=[VMEM] * len(outs),
        scratch_shapes=list(scratch),
        compiler_params=pltpu.CompilerParams(vmem_limit_bytes=limit),
    )(*args)


def solve_small(system, target):
    size = system.shape[0]
    turned = jnp.concatenate([system, target], axis=0)
    rows = [jnp.broadcast_to(turned[:, i : i + 1], (2 * size, 128)) for i in range(size)]
    for p in range(size):
        base = 8 * ((p + 1) // 8)
        lead = [rows[i][p - (2 * size - rows[i].shape[0])][None, :] for i in range(size)]
        keep = base - (2 * size - rows[0].shape[0])
        pivot = rows[p][keep:] / lead[p]
        rows = [
            pivot if i == p else rows[i][keep:] - lead[i] * pivot for i in range(size)
        ]
    return rows


def matrix_turned(rows):
    lanes = lax.broadcasted_iota(jnp.int32, rows[0].shape, 1)
    total = jnp.zeros(rows[0].shape, F32)
    for i, row in enumerate(rows):
        total = jnp.where(lanes == i, row, total)
    return total[:, : len(rows)]


def split_three(gram):
    size = gram.shape[0]
    high = gram.astype(BF16).astype(F32)
    rest = gram - high
    middle = rest.astype(BF16).astype(F32)
    low = rest - middle
    fill = jnp.zeros((size, 128 - 3 * size), F32)
    return jnp.concatenate([high, middle, low, fill], axis=1).astype(BF16)


def join_three(total):
    size = total.shape[0]
    return total[:, :size] + total[:, size : 2 * size] + total[:, 2 * size : 3 * size]


def read_rows(ref):
    return [ref[i] for i in range(ref.shape[0])]


def mix_tile(tile, spread):
    total = None
    for i, factor in enumerate(spread):
        term = factor * tile[i : i + 1, :]
        total = term if total is None else total + term
    return total


def small_dot(first, second, dims):
    return lax.dot_general(
        first, second, (dims, ((), ())), precision=lax.Precision.HIGHEST, preferred_element_type=F32
    )


def halves(value):
    high = value.astype(BF16)
    return high, (value - high.astype(F32)).astype(BF16)


def nt(first, second):
    return lax.dot_general(first, second, (((1,), (1,)), ((), ())), preferred_element_type=F32)


def gram_halves(first, second):
    (fh, fl), (sh, sl) = first, second
    return nt(fh, sh) + (nt(fh, sl) + nt(fl, sh))


def wide(ref, start, count):
    return jnp.concatenate([ref[start + k] for k in range(count)], axis=1)


def each(count, body, step=8):

    def several(start, carry):
        for k in range(step):
            body(start * step + k)
        return carry

    lax.fori_loop(0, count // step, several, 0)


def gram(first, second, unroll=False):
    step = 8

    def add(k, total):
        one = halves(wide(first, k * step, step))
        two = one if second is first else halves(wide(second, k * step, step))
        return total + gram_halves(one, two)

    start = jnp.zeros((first.shape[1], first.shape[1]), F32)
    return lax.fori_loop(0, first.shape[0] // step, add, start, unroll=unroll)


def pack(residual, own_tile, sent, first_plane, last_plane, copies, slots, plane):
    tiles = residual.shape[0]
    blocks = [residual[own_tile[s]].astype(BF16) for s in range(slots)]
    blocks.append(split_three(gram(residual, residual, unroll=True)))
    for m in range(copies):
        for s in range(slots + 1):
            sent[m * (slots + 1) + s] = blocks[s]
    for y in range(plane):
        first_plane[y] = residual[y].astype(BF16)
        last_plane[y] = residual[tiles - plane + y].astype(BF16)


def begin_kernel(copies, slots, plane, own_tile, residual, sent, first_plane, last_plane):
    pack(residual, own_tile, sent, first_plane, last_plane, copies, slots, plane)


def advance(src_count, slots, slot_tile, groups, residual, smooth, norm, image, fresh):
    tiles = residual.shape[0]
    per = slots + 1
    image[pl.ds(0, tiles)] = smooth[...]

    def add_group(i, curvature):
        for s in range(slots):
            tile = slot_tile[i * slots + s]
            image[tile] = image[tile] + groups[i * per + s].astype(F32)
        return curvature + groups[i * per + slots].astype(F32)

    start = jnp.zeros(groups.shape[1:], F32)
    curvature = join_three(lax.fori_loop(0, src_count, add_group, start))
    spread = solve_small(curvature, norm[...])

    def subtract(l):
        fresh[l] = residual[l] - mix_tile(image[l], spread)

    each(tiles, subtract)
    return spread


def step_kernel(
    src_count, copies, slots, plane, slot_tile, own_tile, groups, residual, smooth, norm,
    fresh, alpha_out, sent, first_plane, last_plane, image,
):
    alpha = advance(src_count, slots, slot_tile, groups, residual, smooth, norm, image, fresh)
    for i, row in enumerate(alpha):
        alpha_out[i] = row
    pack(fresh, own_tile, sent, first_plane, last_plane, copies, slots, plane)


def last_kernel(
    src_count, slots, slot_tile, groups, residual, smooth, norm, direction, solution,
    fresh, solution_out, image,
):
    spread = advance(src_count, slots, slot_tile, groups, residual, smooth, norm, image, fresh)

    def add(l):
        solution_out[l] = solution[l] + mix_tile(direction[l], spread)

    each(residual.shape[0], add)


def smooth_field(field, before, after, diagonal, out, plane):
    tiles = field.shape[0]
    lanes = lax.broadcasted_iota(jnp.int32, field.shape[1:], 1)
    last = field.shape[2] - 1
    end = tiles // plane - 1

    def one_plane(x, carry):
        weights = diagonal[pl.ds(pl.multiple_of(x * plane, plane), plane), :]
        for y in range(plane):
            l = x * plane + y
            tile = field[l]
            beside = jnp.where(lanes == 0, 0.0, pltpu.roll(tile, 1, 1))
            beside = beside + jnp.where(lanes == last, 0.0, pltpu.roll(tile, last, 1))
            if y > 0:
                beside = beside + field[l - 1]
            if y < plane - 1:
                beside = beside + field[l + 1]
            lower = field[jnp.maximum(l - plane, y)]
            upper = field[jnp.minimum(l + plane, end * plane + y)]
            beside = beside + jnp.where(x == 0, before[y].astype(F32), lower)
            beside = beside + jnp.where(x == end, after[y].astype(F32), upper)
            out[l] = weights[y : y + 1, :] * tile - beside
        return carry

    lax.fori_loop(0, end + 1, one_plane, 0)


def regularize_first(plane, field, before, after, diagonal, smooth, gram_own, rim_before, rim_after):
    rim_before[...] = before[...].astype(F32)
    rim_after[...] = after[...].astype(F32)
    smooth_field(field, before, after, diagonal, smooth, plane)
    gram_own[...] = gram(field, smooth)


def regularize_kernel(
    plane, field, before, after, diagonal, smooth_old, gram_own, gram_cross, fresh
):
    gram_cross[...] = gram(field, smooth_old)
    smooth_field(field, before, after, diagonal, fresh, plane)
    gram_own[...] = gram(field, fresh)


def data_kernel(first, across_x, cap, share, place, arrived, stored, row_weight, *refs):
    refs, panels, arrival = refs[:-2], refs[-2], refs[-1]
    coming = pltpu.make_async_copy(stored, panels, arrival)
    coming.start()
    if first:
        gram_own, norm_out, response_out, gram_out, outgoing = refs
    else:
        (gram_own, gram_cross, gram_old, norm_old, response_old,
         norm_out, beta_out, response_out, gram_out, outgoing) = refs
    per = cap + 1
    tx_here, rows_here, width = panels.shape
    columns, block_len = arrived.shape[1:]
    foot_len = width // block_len
    total = arrived[cap].astype(F32)
    for x in range(1, across_x):
        total = total + arrived[x * per + cap].astype(F32)
    norm = join_three(total)
    norm_out[...] = norm
    beta = None
    pair = gram_own[...]
    if not first:
        rows = solve_small(norm_old[...], norm)
        for i, row in enumerate(rows):
            beta_out[i] = row
        beta = matrix_turned(rows)
        cross = small_dot(beta, gram_cross[...], ((1,), (1,)))
        inner = small_dot(beta, gram_old[...], ((1,), (0,)))
        pair = pair + cross + cross.T + small_dot(inner, beta, ((1,), (1,)))
    gram_out[...] = pair
    curvature = share * pair
    empty = jnp.zeros((columns, block_len), BF16)
    responses, weights = [], []
    for x in range(across_x):
        for s in range(cap):
            outgoing[x * per + s] = empty
    coming.wait()
    for t in range(tx_here):
        picked = jnp.concatenate([arrived[place[t, f]] for f in range(foot_len)], axis=1)
        response = nt(picked, panels[t])
        if not first:
            response = response + small_dot(beta, response_old[t], ((1,), (0,)))
        response_out[t] = response
        weighted = response * row_weight[t : t + 1, :]
        responses.append(response)
        weights.append(weighted)
    for t in range(tx_here):
        shares = jnp.dot(
            weights[t].astype(BF16), panels[t], preferred_element_type=F32
        ).astype(BF16)
        for f in range(foot_len):
            outgoing[place[t, f]] = shares[:, f * block_len : (f + 1) * block_len]
    curvature = curvature + gram_halves(
        halves(jnp.concatenate(responses, axis=1)), halves(jnp.concatenate(weights, axis=1))
    )
    pieces = split_three(curvature)
    for x in range(across_x):
        outgoing[x * per + cap] = pieces


def mix_kernel(
    plane, fresh, before, after, diagonal, direction, rim_before, rim_after, beta,
    direction_out, smooth_out, rim_before_out, rim_after_out,
):
    spread = read_rows(beta)

    def inside(l):
        direction_out[l] = fresh[l] + mix_tile(direction[l], spread)

    def beside(y):
        rim_before_out[y] = before[y].astype(F32) + mix_tile(rim_before[y], spread)
        rim_after_out[y] = after[y].astype(F32) + mix_tile(rim_after[y], spread)

    each(fresh.shape[0], inside)
    each(plane, beside, 4)
    smooth_field(direction_out, rim_before_out, rim_after_out, diagonal, smooth_out, plane)


def gather_kernel(*refs):
    count = (len(refs) - 1) // 2
    directions, alphas, out = refs[:count], refs[count : 2 * count], refs[-1]
    spreads = [read_rows(alpha) for alpha in alphas]
    for k in range(count):

        def add(l):
            term = mix_tile(directions[k][l], spreads[k])
            out[l] = term if k == 0 else out[l] + term

        each(out.shape[0], add)


def narrow_kernel(across_x, inner, slots, cap, kept, across, out):
    per = slots + 1
    total = across[slots].astype(F32)
    for y in range(1, inner):
        total = total + across[y * per + slots].astype(F32)
    pieces = split_three(join_three(total))
    for x in range(across_x):
        out[x * (cap + 1) + cap] = pieces
    for d in range(cap):
        block = across[kept[d]]
        for x in range(across_x):
            out[x * (cap + 1) + d] = block


def widen_kernel(across_x, inner, slots, cap, kept, incoming, out):
    per = slots + 1
    empty = jnp.zeros(out.shape[1:], BF16)
    for s in range(inner * per):
        out[s] = empty

    def summed(d):
        total = incoming[d].astype(F32)
        for x in range(1, across_x):
            total = total + incoming[x * (cap + 1) + d].astype(F32)
        return total

    for d in range(cap):
        out[kept[d]] = summed(d).astype(BF16)
    pieces = split_three(join_three(summed(cap)))
    for y in range(inner):
        out[y * per + slots] = pieces


def sum_kernel(copies, slots, incoming, handed):
    per = slots + 1
    for s in range(per):
        total = incoming[s].astype(F32)
        for m in range(1, copies):
            total = total + incoming[m * per + s].astype(F32)
        handed[s] = total.astype(BF16) if s < slots else split_three(join_three(total))


def owners_ranks(tile_ids, blocks_dev):
    owners = tile_ids // blocks_dev
    position = jnp.arange(tile_ids.shape[1])
    before = (owners[:, :, None] == owners[:, None, :]) & (
        position[None, None, :] < position[None, :, None]
    )
    ranking = jnp.sum(before.astype(jnp.int32), axis=2)
    return (owners, tile_ids - owners * blocks_dev, ranking)


def shards(right_side, depth_weight, panels, data_weight, footprints, counts):
    columns, extent_x, extent_y, block_len = right_side.shape
    tx_here, rows_here, foot_len, _ = panels.shape
    copies = lax.axis_size("mod")
    src_count = lax.axis_size("src")
    tiles = extent_x * extent_y
    plane = extent_y
    slots = tx_here * CAP
    per = slots + 1
    mod_index = lax.axis_index("mod")
    src_index = lax.axis_index("src")
    group_counts = lax.dynamic_slice_in_dim(counts, src_index * tx_here, tx_here, 0)
    group = lax.dynamic_slice_in_dim(footprints, src_index * tx_here, tx_here, 0)
    owners, _, ranking = owners_ranks(group, tiles)

    def tiles_of_slots(tile_ids):
        its_owners, within, its_ranking = owners_ranks(tile_ids, tiles)
        chosen = (its_owners == mod_index)[:, None, :] & (
            its_ranking[:, None, :] == jnp.arange(CAP)[None, :, None]
        )
        return jnp.min(jnp.where(chosen, within[:, None, :], tiles), axis=2).reshape(-1)

    own_tile = jnp.minimum(tiles_of_slots(group), tiles - 1)
    row_ids = mod_index * rows_here + jnp.arange(rows_here)
    row_weight = data_weight * (row_ids[None, :] < group_counts[:, None]).astype(F32)
    up = [(i, i + 1) for i in range(copies - 1)]
    down = [(i + 1, i) for i in range(copies - 1)]
    flat_panels = lax.optimization_barrier(
        panels.reshape(tx_here, rows_here, foot_len * block_len)
    )
    diagonal = 6.0 + depth_weight.reshape(tiles, block_len)
    share = 1.0 / src_count
    inner = INNER
    across_x = copies // inner
    along_y = [[x * inner + y for y in range(inner)] for x in range(across_x)]
    along_x = [[x * inner + y for x in range(across_x)] for y in range(inner)]

    field = ((tiles, columns, block_len), F32)
    small = ((columns, columns), F32)
    edge = ((plane, columns, block_len), BF16)
    factors = ((columns, columns, 128), F32)
    rim = ((plane, columns, block_len), F32)
    part = ((inner * per, columns, block_len), BF16)

    responses = ((tx_here, columns, rows_here), F32)
    image = pltpu.VMEM((tiles + 1, columns, block_len), F32)
    panel_room = (
        pltpu.VMEM((tx_here, rows_here, foot_len * block_len), BF16),
        pltpu.SemaphoreType.DMA(()),
    )
    own_slots = owners * slots + jnp.arange(tx_here)[:, None] * CAP + ranking
    used = jnp.any(
        own_slots.reshape(-1)[:, None] == jnp.arange(copies * slots)[None, :], axis=0
    ).reshape(across_x, inner * slots)
    rank_used = jnp.cumsum(used.astype(jnp.int32), axis=1) - 1
    x_of = footprints // (tiles * inner)
    filled = jnp.sum(
        (x_of.reshape(src_count, -1)[:, :, None] == jnp.arange(across_x)[None, None, :]).astype(
            jnp.int32
        ),
        axis=1,
    )
    all_slots = inner * slots

    def places(cap):
        at = jnp.sum(
            jnp.where(
                own_slots[:, :, None] == jnp.arange(copies * slots)[None, None, :],
                rank_used.reshape(-1)[None, None, :],
                0,
            ),
            axis=2,
        )
        place = (owners // inner) * (cap + 1) + at
        here = mod_index // inner
        used_here = lax.dynamic_index_in_dim(used, here, 0, keepdims=False)
        rank_here = lax.dynamic_index_in_dim(rank_used, here, 0, keepdims=False)
        slot = jnp.arange(all_slots)
        slot = (slot // slots) * per + slot % slots
        match = used_here[None, :] & (rank_here[None, :] == jnp.arange(cap)[:, None])
        kept = jnp.sum(jnp.where(match, slot[None, :], 0), axis=1)
        kept = jnp.where(jnp.any(match, axis=1), kept, slots)
        return place, kept

    residual = right_side.transpose(1, 2, 0, 3).reshape(field[0])
    sent, first_plane, last_plane = call(
        functools.partial(begin_kernel, inner, slots, plane),
        [part, edge, edge],
        (own_tile, residual),
        (SMEM, VMEM),
    )
    def to_field(parts):
        return parts.reshape(extent_x, extent_y, columns, block_len).transpose(2, 0, 1, 3)

    def along(sent, first_plane, last_plane):
        across = lax.all_to_all(sent, "mod", 0, 0, tiled=True, axis_index_groups=along_y)
        before = lax.ppermute(last_plane, "mod", up)
        after = lax.ppermute(first_plane, "mod", down)
        return across, before, after

    def iterations(cap, residual, across, before, after):
        packet = ((across_x * (cap + 1), columns, block_len), BF16)
        place, kept = places(cap)
        place, slot_tile = lax.optimization_barrier((place, tiles_of_slots(footprints)))

        def reduced(outgoing):
            halfway = lax.all_to_all(
                outgoing, "mod", 0, 0, tiled=True, axis_index_groups=along_x
            )
            (halfway,) = call(
                functools.partial(widen_kernel, across_x, inner, slots, cap),
                [part],
                (kept, halfway),
                (SMEM, VMEM),
            )
            return lax.all_to_all(halfway, "mod", 0, 0, tiled=True, axis_index_groups=along_y)

        direction = smooth = norm = response = gram_pair = rim_before = rim_after = None
        directions, alphas = [], []
        for iteration in range(ITERS):
            if iteration > 0:
                across, before, after = along(sent, first_plane, last_plane)
            (narrow,) = call(
                functools.partial(narrow_kernel, across_x, inner, slots, cap),
                [packet],
                (kept, across),
                (SMEM, VMEM),
            )
            arrived = lax.all_to_all(
                narrow, "mod", 0, 0, tiled=True, axis_index_groups=along_x
            )
            if iteration == 0:
                smooth, gram_own, rim_before, rim_after = call(
                    functools.partial(regularize_first, plane),
                    [field, small, rim, rim],
                    (residual, before, after, diagonal),
                    (VMEM,) * 4,
                )
                direction = residual
                norm, response, gram_pair, outgoing = call(
                    functools.partial(data_kernel, True, across_x, cap, share),
                    [small, responses, small, packet],
                    (place, arrived, flat_panels, row_weight, gram_own),
                    (SMEM, VMEM, ANY) + (VMEM,) * 2,
                    scratch=panel_room,
                )
                incoming = reduced(outgoing)
            else:
                gram_own, gram_cross = call(
                    functools.partial(regularize_kernel, plane),
                    [small, small],
                    (residual, before, after, diagonal, smooth),
                    (VMEM,) * 5,
                    scratch=(pltpu.VMEM(field[0], F32),),
                )
                norm, beta, response, gram_pair, outgoing = call(
                    functools.partial(data_kernel, False, across_x, cap, share),
                    [small, factors, responses, small, packet],
                    (place, arrived, flat_panels, row_weight, gram_own, gram_cross,
                     gram_pair, norm, response),
                    (SMEM, VMEM, ANY) + (VMEM,) * 6,
                    scratch=panel_room,
                )
                incoming = reduced(outgoing)
                direction, smooth, rim_before, rim_after = call(
                    functools.partial(mix_kernel, plane),
                    [field, field, rim, rim],
                    (residual, before, after, diagonal,
                     direction, rim_before,
                     rim_after, beta),
                    (VMEM,) * 8,
                )
            directions.append(direction)
            if iteration + 1 == ITERS:
                (solution,) = call(
                    gather_kernel,
                    [field],
                    (*directions[:-1],
                     *alphas),
                    (VMEM,) * (2 * len(alphas)),
                )
            (handed,) = call(
                functools.partial(sum_kernel, inner, slots),
                [((per, columns, block_len), BF16)],
                (incoming,),
                (VMEM,),
            )
            groups = lax.all_gather(handed, "src", axis=0, tiled=True)
            if iteration + 1 < ITERS:
                residual, alpha, sent, first_plane, last_plane = call(
                    functools.partial(step_kernel, src_count, inner, slots, plane),
                    [field, factors, part, edge, edge],
                    (slot_tile, own_tile, groups, residual, smooth, norm),
                    (SMEM, SMEM) + (VMEM,) * 4,
                    scratch=(image,),
                )
                alphas.append(alpha)
            else:
                residual, solution = call(
                    functools.partial(last_kernel, src_count, slots),
                    [field, field],
                    (slot_tile, groups, residual, smooth, norm, direction,
                     solution),
                    (SMEM,) + (VMEM,) * 6,
                    scratch=(image,),
                )
        return to_field(solution), to_field(residual)

    across, before, after = along(sent, first_plane, last_plane)
    solution, residual = lax.cond(
        jnp.all(filled <= NARROW),
        functools.partial(iterations, NARROW),
        functools.partial(iterations, all_slots),
        residual,
        across,
        before,
        after,
    )

    return solution, residual


def solution(mesh):
    placed = (
        P(None, "mod", None, None),
        P("mod", None, None),
        P("src", "mod", None, None),
        P("src", "mod"),
        P(),
        P(),
    )
    return jax.shard_map(
        shards,
        mesh=mesh,
        in_specs=placed,
        out_specs=(P(None, "mod", None, None), P(None, "mod", None, None)),
        check_vma=False,
    )
```
